32 devices in a mesh: blk: 8 (over z, x), rep: 4 (over y, core).
Axes of the slice: x: 2, y: 2, z: 4, core: 2. Of those that a mesh axis runs over, the one named last changes fastest.
Arguments:
- pixel_factors: float32 [24576, 256], P(('blk', 'rep')), may hold values from -1.5 to 1.5
- scene_factors: float32 [8192, 256], P('blk'), may hold values from -1.5 to 1.5
- elevations: bfloat16 [3, 24576, 1024], P(None, ('blk', 'rep')), may hold values from -6 to 6
- quality: bfloat16 [3, 24576, 1024], P(None, ('blk', 'rep')), may hold values from 0 to 1, as said below
- occupancy: int32 [3, 32], P(None, ('blk', 'rep')), may hold values from 0 to 1, as said below
Outputs:
- pixel_out: float32 [24576, 256], P(('blk', 'rep'))
- scene_out: float32 [8192, 256], P('blk')
The draws below stay inside these ranges and needn't reach their ends.
Inputs may be any that keep to these rules, and one draw needn't show every extreme that they name: quality is zero on every entry of an owner's tile whose occupancy is 0; otherwise about half of the entries are nonzero. occupancy is 0 or 1 and about three quarters of the tiles are occupied.
All inputs are finite; a program needn't handle non-finite values.
Results may differ from the reference program's by a relative error of at most 0.0003.
Values sent between devices are 32-bit elements; how exact they have to be, the bound alone decides.
A program may use at most 64 MiB of HBM per device.

```python
import jax
import jax.numpy as jnp
from jax import lax

PIX_DEV = 768
ACQ_BLK = 1024
R = 256
STEPS = 3
PIX = 24576
ACQ = 8192
OWNERS = 32
GROUP_ROWS = 3072
N_BLK = 8


def occupied_tiles(key):
    tile_key = jax.random.fold_in(key, 11)
    return (jax.random.randint(tile_key, (STEPS, OWNERS), 0, 4) < 3).astype(jnp.int32)


def draw_occupancy(key, part):
    return occupied_tiles(key)


def draw_quality(key, part):
    owner_flags = occupied_tiles(key)
    seen = (jax.random.randint(jax.random.fold_in(key, 23), (STEPS, PIX, ACQ_BLK), 0, 20) < 11).astype(jnp.float32)
    mag_key = jax.random.fold_in(key, 37)
    magnitude = jax.random.uniform(mag_key, (STEPS, PIX, ACQ_BLK), jnp.float32, 0.2, 1.0)
    owner_rows = jnp.repeat(owner_flags.astype(jnp.float32), PIX_DEV, axis=1)
    return (magnitude * seen * owner_rows[:, :, None]).astype(jnp.bfloat16)


def block_levels(stream_key, shape, cuts, least, largest):
    gain, own = 1.0, jax.random.fold_in(stream_key, 6)
    for dim, parts in cuts:
        steps = jnp.exp(jax.random.uniform(jax.random.fold_in(own, dim), (parts,), jnp.float32, least / len(cuts), largest / len(cuts)))
        gain = gain * jnp.repeat(steps, shape[dim] // parts).reshape([-1 if axis == dim else 1 for axis in range(len(shape))])
    return gain


def noise(stream_key, dims, deviation, reach, shards=(), held_as=jnp.bfloat16):
    loudness = block_levels(stream_key, dims, shards, -0.22, 0.18) if shards else 1.0
    drawn = jax.random.normal(stream_key, dims, jnp.float32) * deviation * loudness
    return jnp.minimum(jnp.maximum(drawn, -reach), reach).astype(held_as)


def setup_inputs(seed: int = 0) -> dict:
    seeds = jax.random.split(jax.random.key(seed), 6)
    return {
        "pixel_factors": noise(seeds[0], (PIX, R), 0.25, 1.5, ((0, 32),), jnp.float32),
        "scene_factors": noise(seeds[1], (ACQ, R), 0.25, 1.5, ((0, 8),), jnp.float32),
        "elevations": noise(seeds[2], (STEPS, PIX, ACQ_BLK), 1.0, 6.0, ((1, 32),)),
        "quality": draw_quality(jax.random.fold_in(seeds[5], 71), 0),
        "occupancy": draw_occupancy(jax.random.fold_in(seeds[5], 71), 0),
    }


def group_update(args):
    pixel_rows, scene_block, tile_values, tile_quality, owner_flag = args
    weight = tile_quality.astype(jnp.float32) * owner_flag[:, None]
    predicted = jnp.dot(pixel_rows, scene_block.T, precision=lax.Precision.HIGHEST, preferred_element_type=jnp.float32)
    misfit = weight * (tile_values.astype(jnp.float32) - predicted)
    pixel_grad = jnp.dot(misfit, scene_block, precision=lax.Precision.HIGHEST, preferred_element_type=jnp.float32)
    scene_grad = jnp.dot(misfit.T, pixel_rows, precision=lax.Precision.HIGHEST, preferred_element_type=jnp.float32)
    new_pixels = pixel_rows + (8.0 / ACQ_BLK) * pixel_grad
    new_scene = scene_block + (8.0 / GROUP_ROWS) * scene_grad
    return new_pixels, new_scene


def reference(pixel_factors, scene_factors, elevations, quality, occupancy):
    pixels = pixel_factors.reshape(N_BLK, GROUP_ROWS, R)
    scenes = scene_factors.reshape(N_BLK, ACQ_BLK, R)
    owner_rows = jnp.repeat(occupancy.astype(jnp.float32), PIX_DEV, axis=1).reshape(STEPS, N_BLK, GROUP_ROWS)
    tiles = elevations.reshape(STEPS, N_BLK, GROUP_ROWS, ACQ_BLK)
    weights = quality.reshape(STEPS, N_BLK, GROUP_ROWS, ACQ_BLK)
    for step_index in range(STEPS):
        paired = jnp.roll(scenes, -step_index, axis=0)
        pixels, paired = lax.map(group_update, (pixels, paired, tiles[step_index], weights[step_index], owner_rows[step_index]))
        scenes = jnp.roll(paired, step_index, axis=0)
    return pixels.reshape(PIX, R), scenes.reshape(ACQ, R)
```

```python
import functools

import jax
import jax.numpy as jnp
from jax import lax
from jax.experimental import pallas as pl
from jax.experimental.pallas import tpu as pltpu
from jax.sharding import PartitionSpec as P

MESH = pl.DeviceIdType.MESH
STEPS = 3
CHUNK = 128
PAIR = 256
ROWS = 256
LAG_SUM = 1
LAG_UPDATE = 3
LAG_FORWARD = 5


def split(value):
    high = value.astype(jnp.bfloat16)
    return high, (value - high.astype(jnp.float32)).astype(jnp.bfloat16)


def dot(left, right):
    return jnp.dot(left, right, preferred_element_type=jnp.float32)


def kernel(
    blk_count, rep_count,
    occ_ref, pix_ref, scene_ref, elev_ref, qual_ref, pix_out, scene_out,
    elev, qual, u_ref, p_ref, u_cat, ut_high, ut_low, v_all, v_high, v_low, m_high, m_low,
    grad, core_in, chip_sum, fresh,
    load_sem, tile_sem, core_send, core_recv, chip_send, chip_recv, move_send, move_recv, fwd_send, fwd_recv,
):
    pixels, rank = pix_ref.shape
    acq = scene_ref.shape[0]
    per_step = acq // CHUNK
    total = STEPS * per_step
    half = CHUNK // 2
    chips = rep_count // 2
    pixel_rate = 8.0 / acq
    scene_rate = 8.0 / (pixels * rep_count)

    group = lax.axis_index("blk")
    rep = lax.axis_index("rep")
    core = lax.rem(rep, 2)
    chip = lax.div(rep, 2)
    other_core = chip * 2 + 1 - core

    load_u = pltpu.make_async_copy(pix_ref, u_ref, load_sem.at[0])
    load_v = pltpu.make_async_copy(scene_ref, v_all.at[0], load_sem.at[1])
    load_u.start()
    load_v.start()

    def tile_loads(step):
        return (
            pltpu.make_async_copy(elev_ref.at[step], elev.at[step], tile_sem.at[0, step]),
            pltpu.make_async_copy(qual_ref.at[step], qual.at[step], tile_sem.at[1, step]),
        )

    for step in range(STEPS):
        for load in tile_loads(step):
            load.start()

    def at_blk(shift):
        return lax.rem(group + shift + blk_count, blk_count)

    barrier = pltpu.get_barrier_semaphore()
    partners = [(group, other_core)]
    for offset in range(1, chips):
        partners.append((group, lax.rem(chip + offset, chips) * 2 + core))
    for shift in (-1, 1, STEPS - 1, 1 - STEPS):
        partners.append((at_blk(shift), rep))
    for partner in partners:
        pl.semaphore_signal(barrier, inc=1, device_id=partner, device_id_type=MESH)

    p_ref[...] = jnp.zeros_like(p_ref)
    load_u.wait()
    load_v.wait()
    pl.semaphore_wait(barrier, len(partners))

    def core_copy(n):
        return pltpu.make_async_remote_copy(
            src_ref=grad.at[n, pl.ds(pl.multiple_of((1 - core) * half, half), half)],
            dst_ref=core_in.at[n],
            send_sem=core_send.at[n], recv_sem=core_recv.at[n],
            device_id=(group, other_core), device_id_type=MESH,
        )

    def chip_copy(n, offset):
        return pltpu.make_async_remote_copy(
            src_ref=chip_sum.at[n, chip], dst_ref=chip_sum.at[n, chip],
            send_sem=chip_send.at[n, offset - 1], recv_sem=chip_recv.at[n, chip],
            device_id=(group, lax.rem(chip + offset, chips) * 2 + core), device_id_type=MESH,
        )

    def chip_arrival(n, offset):
        sender = lax.rem(chip + offset, chips)
        return pltpu.make_async_remote_copy(
            src_ref=chip_sum.at[n, sender], dst_ref=chip_sum.at[n, sender],
            send_sem=chip_send.at[n, offset - 1], recv_sem=chip_recv.at[n, sender],
            device_id=(group, sender * 2 + core), device_id_type=MESH,
        )

    def place(n, side):
        step = lax.div(n, per_step)
        start = lax.rem(n, per_step) * CHUNK + side * half
        return v_all.at[step + 1, pl.ds(pl.multiple_of(start, half), half)]

    def move_copy(n):
        last = lax.div(lax.div(n, per_step), STEPS - 1)
        return pltpu.make_async_remote_copy(
            src_ref=fresh.at[n], dst_ref=place(n, core),
            send_sem=move_send.at[n], recv_sem=move_recv.at[n],
            device_id=(at_blk(last * STEPS - 1), rep), device_id_type=MESH,
        )

    def forward_copy(n):
        return pltpu.make_async_remote_copy(
            src_ref=place(n, core), dst_ref=place(n, core),
            send_sem=fwd_send.at[n], recv_sem=fwd_recv.at[n],
            device_id=(group, other_core), device_id_type=MESH,
        )

    def forward_arrival(n):
        return pltpu.make_async_remote_copy(
            src_ref=place(n, 1 - core), dst_ref=place(n, 1 - core),
            send_sem=fwd_send.at[n], recv_sem=fwd_recv.at[n],
            device_id=(group, other_core), device_id_type=MESH,
        )

    def begin_step(step):
        for load in tile_loads(step):
            load.wait()
        for start in range(0, pixels, ROWS):
            rows = pl.ds(start, ROWS)
            u = u_ref[rows, :] + pixel_rate * p_ref[rows, :]
            u_ref[rows, :] = u
            p_ref[rows, :] = jnp.zeros_like(u)
            high, low = split(u)
            u_cat[rows, :] = jnp.concatenate([high, high, low], axis=1)
            high, low = split(u.T)
            ut_high[:, rows] = high
            ut_low[:, rows] = low

    def work(n):
        step = lax.div(n, per_step)
        first = pl.multiple_of(lax.rem(n, per_step) * CHUNK, CHUNK)
        cols = pl.ds(first, CHUNK)
        flag = occ_ref[step, 0].astype(jnp.float32)
        v = v_all[step, cols, :]
        high, low = split(v)
        v_high[cols, :] = high
        v_low[cols, :] = low
        high, low = split(v.T)
        v_cat = jnp.concatenate([high, low, high], axis=0)
        for start in range(0, pixels, ROWS):
            rows = pl.ds(start, ROWS)
            predicted = dot(u_cat[rows, :], v_cat)
            weight = qual[step, rows, cols].astype(jnp.float32) * flag
            misfit = weight * (elev[step, rows, cols].astype(jnp.float32) - predicted)
            high, low = split(misfit)
            m_high[rows, cols] = high
            m_low[rows, cols] = low
        high = m_high[:, cols]
        turned = dot(ut_high[...], high) + dot(ut_high[...], m_low[:, cols]) + dot(ut_low[...], high)
        grad[n] = turned.T

    def add_pixel_grad(n):
        first = pl.multiple_of(lax.rem(n, per_step) * CHUNK + CHUNK - PAIR, PAIR)
        cols = pl.ds(first, PAIR)
        high, low = v_high[cols, :], v_low[cols, :]
        v_cat = jnp.concatenate([high, high, low], axis=0)
        for start in range(0, pixels, ROWS):
            rows = pl.ds(start, ROWS)
            high, low = m_high[rows, cols], m_low[rows, cols]
            p_ref[rows, :] += dot(jnp.concatenate([high, low, high], axis=1), v_cat)

    def tick(t, carry):
        @pl.when(t < total)
        def _():
            @pl.when(lax.rem(t, per_step) == 0)
            def _():
                begin_step(lax.div(t, per_step))

            @pl.when(t >= per_step)
            def _():
                forward_arrival(t - per_step).wait_recv()

            work(t)
            core_copy(t).start()

            @pl.when(lax.rem(lax.rem(t, per_step) * CHUNK + CHUNK, PAIR) == 0)
            def _():
                add_pixel_grad(t)

        n_sum = t - LAG_SUM

        @pl.when(jnp.logical_and(n_sum >= 0, n_sum < total))
        def _():
            core_copy(n_sum).wait_recv()
            own = grad[n_sum, pl.ds(pl.multiple_of(core * half, half), half), :]
            chip_sum[n_sum, chip] = own + core_in[n_sum]
            for offset in range(1, chips):
                chip_copy(n_sum, offset).start()

        n_new = t - LAG_UPDATE

        @pl.when(jnp.logical_and(n_new >= 0, n_new < total))
        def _():
            for offset in range(1, chips):
                chip_arrival(n_new, offset).wait_recv()
            summed = chip_sum[n_new, 0]
            for index in range(1, chips):
                summed = summed + chip_sum[n_new, index]
            start = lax.rem(n_new, per_step) * CHUNK + core * half
            old = v_all[lax.div(n_new, per_step), pl.ds(pl.multiple_of(start, half), half), :]
            fresh[n_new] = old + scene_rate * summed
            move_copy(n_new).start()

        n_fwd = t - LAG_FORWARD

        @pl.when(jnp.logical_and(n_fwd >= 0, n_fwd < total))
        def _():
            move_copy(n_fwd).wait_recv()
            forward_copy(n_fwd).start()

        return carry

    lax.fori_loop(0, total + LAG_FORWARD, tick, 0)

    for start in range(0, pixels, ROWS):
        rows = pl.ds(start, ROWS)
        pix_out[rows, :] = u_ref[rows, :] + pixel_rate * p_ref[rows, :]

    def finish(c, carry):
        forward_arrival((STEPS - 1) * per_step + c).wait_recv()
        cols = pl.ds(pl.multiple_of(c * CHUNK, CHUNK), CHUNK)
        scene_out[cols, :] = v_all[STEPS, cols, :]
        return carry

    lax.fori_loop(0, per_step, finish, 0)

    def drain(n, carry):
        core_copy(n).wait_send()
        for offset in range(1, chips):
            chip_copy(n, offset).wait_send()
        move_copy(n).wait_send()
        forward_copy(n).wait_send()
        return carry

    lax.fori_loop(0, total, drain, 0)


def per_device(blk_count, rep_count, pixel_factors, scene_factors, elevations, quality, occupancy):
    pixels, rank = pixel_factors.shape
    acq = scene_factors.shape[0]
    total = STEPS * (acq // CHUNK)
    half = CHUNK // 2
    chips = rep_count // 2
    f32, bf16 = jnp.float32, jnp.bfloat16
    anywhere = pl.BlockSpec(memory_space=pl.ANY)
    in_vmem = pl.BlockSpec(memory_space=pltpu.VMEM)
    dma = pltpu.SemaphoreType.DMA
    return pl.pallas_call(
        functools.partial(kernel, blk_count, rep_count),
        out_shape=(
            jax.ShapeDtypeStruct((pixels, rank), f32),
            jax.ShapeDtypeStruct((acq, rank), f32),
        ),
        in_specs=[pl.BlockSpec(memory_space=pltpu.SMEM)] + [anywhere] * 4,
        out_specs=(in_vmem, in_vmem),
        scratch_shapes=[
            pltpu.VMEM(elevations.shape, bf16),
            pltpu.VMEM(quality.shape, bf16),
            pltpu.VMEM((pixels, rank), f32),
            pltpu.VMEM((pixels, rank), f32),
            pltpu.VMEM((pixels, 3 * rank), bf16),
            pltpu.VMEM((rank, pixels), bf16),
            pltpu.VMEM((rank, pixels), bf16),
            pltpu.VMEM((STEPS + 1, acq, rank), f32),
            pltpu.VMEM((acq, rank), bf16),
            pltpu.VMEM((acq, rank), bf16),
            pltpu.VMEM((pixels, acq), bf16),
            pltpu.VMEM((pixels, acq), bf16),
            pltpu.VMEM((total, CHUNK, rank), f32),
            pltpu.VMEM((total, half, rank), f32),
            pltpu.VMEM((total, chips, half, rank), f32),
            pltpu.VMEM((total, half, rank), f32),
            dma((2,)),
            dma((2, STEPS)),
            dma((total,)),
            dma((total,)),
            dma((total, chips)),
            dma((total, chips)),
            dma((total,)),
            dma((total,)),
            dma((total,)),
            dma((total,)),
        ],
        compiler_params=pltpu.CompilerParams(
            collective_id=0, has_side_effects=True, vmem_limit_bytes=56 * 1024 * 1024
        ),
        cost_estimate=pl.CostEstimate(
            flops=18 * STEPS * pixels * acq * rank, bytes_accessed=12 * 1024 * 1024, transcendentals=0
        ),
    )(occupancy, pixel_factors, scene_factors, elevations, quality)


def solution(mesh):
    in_specs = (
        P(("blk", "rep"), None),
        P("blk", None),
        P(None, ("blk", "rep"), None),
        P(None, ("blk", "rep"), None),
        P(None, ("blk", "rep")),
    )
    out_specs = (P(("blk", "rep"), None), P("blk", None))
    return jax.shard_map(
        functools.partial(per_device, mesh.shape["blk"], mesh.shape["rep"]),
        mesh=mesh, in_specs=in_specs, out_specs=out_specs, check_vma=False,
    )
```

```python
import functools

import jax
import jax.numpy as jnp
from jax import lax
from jax.experimental import pallas as pl
from jax.experimental.pallas import tpu as pltpu
from jax.sharding import PartitionSpec as P

MESH = pl.DeviceIdType.MESH
STEPS = 3
CHUNK = 128
PAIR = 256
ROWS = 256
VMEM_BYTES = 56 * 1024 * 1024
LAG_SUM = 1
LAG_UPDATE = 3
LAG_FORWARD = 6


def split(value):
    high = value.astype(jnp.bfloat16)
    return high, (value - high.astype(jnp.float32)).astype(jnp.bfloat16)


def dot(left, right):
    return jnp.dot(left, right, preferred_element_type=jnp.float32)


def kernel(
    blk_count, rep_count,
    occ_ref, pix_ref, scene_ref, elev_ref, qual_ref, pix_out, scene_out,
    elev, qual, u_ref, p_ref, u_parts, ut_parts, v_all, v_high, v_low, m_high, m_low,
    grad, core_in, chip_sum, fresh,
    load_sem, out_sem, tile_sem, core_send, core_recv, chip_send, chip_recv, move_send, move_recv, fwd_send, fwd_recv,
):
    pixels, rank = pix_ref.shape
    acq = scene_ref.shape[0]
    per_step = acq // CHUNK
    total = STEPS * per_step
    half = CHUNK // 2
    chips = rep_count // 2
    pixel_rate = 8.0 / acq
    scene_rate = 8.0 / (pixels * rep_count)

    group = lax.axis_index("blk")
    rep = lax.axis_index("rep")
    core = lax.rem(rep, 2)
    chip = lax.div(rep, 2)
    other_core = chip * 2 + 1 - core

    def at_blk(shift):
        return lax.rem(group + shift + blk_count, blk_count)

    barrier = pltpu.get_barrier_semaphore()
    partners = [(group, other_core)]
    for offset in range(1, chips):
        partners.append((group, lax.rem(chip + offset, chips) * 2 + core))
    for shift in (-1, 1, STEPS - 1, 1 - STEPS):
        partners.append((at_blk(shift), rep))
    for partner in partners:
        pl.semaphore_signal(barrier, inc=1, device_id=partner, device_id_type=MESH)

    load_u = pltpu.make_async_copy(pix_ref, u_ref, load_sem.at[0])
    load_v = pltpu.make_async_copy(scene_ref, v_all.at[0], load_sem.at[1])
    load_u.start()
    load_v.start()

    def tile_loads(step):
        return (
            pltpu.make_async_copy(elev_ref.at[step], elev.at[step], tile_sem.at[0, step]),
            pltpu.make_async_copy(qual_ref.at[step], qual.at[step], tile_sem.at[1, step]),
        )

    for load in tile_loads(0):
        load.start()

    p_ref[...] = jnp.zeros_like(p_ref)
    load_u.wait()
    load_v.wait()

    def core_copy(n):
        return pltpu.make_async_remote_copy(
            src_ref=grad.at[n, pl.ds(pl.multiple_of((1 - core) * half, half), half)],
            dst_ref=core_in.at[n],
            send_sem=core_send.at[n], recv_sem=core_recv.at[n],
            device_id=(group, other_core), device_id_type=MESH,
        )

    def chip_copy(n, offset):
        return pltpu.make_async_remote_copy(
            src_ref=chip_sum.at[n, chip], dst_ref=chip_sum.at[n, chip],
            send_sem=chip_send.at[n, offset - 1], recv_sem=chip_recv.at[n, chip],
            device_id=(group, lax.rem(chip + offset, chips) * 2 + core), device_id_type=MESH,
        )

    def chip_arrival(n, offset):
        sender = lax.rem(chip + offset, chips)
        return pltpu.make_async_remote_copy(
            src_ref=chip_sum.at[n, sender], dst_ref=chip_sum.at[n, sender],
            send_sem=chip_send.at[n, offset - 1], recv_sem=chip_recv.at[n, sender],
            device_id=(group, sender * 2 + core), device_id_type=MESH,
        )

    def place(n, side):
        step = lax.div(n, per_step)
        start = lax.rem(n, per_step) * CHUNK + side * half
        return v_all.at[step + 1, pl.ds(pl.multiple_of(start, half), half)]

    def move_copy(n):
        last = lax.div(lax.div(n, per_step), STEPS - 1)
        return pltpu.make_async_remote_copy(
            src_ref=fresh.at[n], dst_ref=place(n, core),
            send_sem=move_send.at[n], recv_sem=move_recv.at[n],
            device_id=(at_blk(last * STEPS - 1), rep), device_id_type=MESH,
        )

    def forward_copy(n):
        return pltpu.make_async_remote_copy(
            src_ref=place(n, core), dst_ref=place(n, core),
            send_sem=fwd_send.at[n], recv_sem=fwd_recv.at[n],
            device_id=(group, other_core), device_id_type=MESH,
        )

    def forward_arrival(n):
        return pltpu.make_async_remote_copy(
            src_ref=place(n, 1 - core), dst_ref=place(n, 1 - core),
            send_sem=fwd_send.at[n], recv_sem=fwd_recv.at[n],
            device_id=(group, other_core), device_id_type=MESH,
        )

    def begin_step(step):
        for load in tile_loads(step):
            load.wait()

        @pl.when(step + 1 < STEPS)
        def _():
            for load in tile_loads(step + 1):
                load.start()

        for start in range(0, pixels, ROWS):
            rows = pl.ds(start, ROWS)
            u = u_ref[rows, :] + pixel_rate * p_ref[rows, :]
            u_ref[rows, :] = u
            p_ref[rows, :] = jnp.zeros_like(u)
            high, low = split(u)
            u_parts[0, rows, :] = high
            u_parts[1, rows, :] = low
            high, low = split(u.T)
            ut_parts[pl.ds(0, rank), rows] = high
            ut_parts[pl.ds(rank, rank), rows] = low

    def work(n):
        step = lax.div(n, per_step)
        first = pl.multiple_of(lax.rem(n, per_step) * CHUNK, CHUNK)
        cols = pl.ds(first, CHUNK)
        flag = occ_ref[0, step].astype(jnp.float32)
        v = v_all[step, cols, :]
        high, low = split(v)
        v_high[cols, :] = high
        v_low[cols, :] = low
        high, low = split(v.T)
        v_cat = jnp.concatenate([high, low], axis=1)
        for start in range(0, pixels, ROWS):
            rows = pl.ds(start, ROWS)
            by_high = dot(u_parts[0, rows, :], v_cat)
            by_low = dot(u_parts[1, rows, :], v_cat)
            predicted = by_high[:, :CHUNK] + (by_high[:, CHUNK:] + by_low[:, :CHUNK] + by_low[:, CHUNK:])
            weight = qual[step, rows, cols].astype(jnp.float32) * flag
            misfit = weight * (elev[step, rows, cols].astype(jnp.float32) - predicted)
            high, low = split(misfit)
            m_high[rows, cols] = high
            m_low[rows, cols] = low
        parts = dot(ut_parts[...], jnp.concatenate([m_high[:, cols], m_low[:, cols]], axis=1))
        by_high, by_low = parts[:rank], parts[rank:]
        turned = by_high[:, :CHUNK] + (by_high[:, CHUNK:] + by_low[:, :CHUNK] + by_low[:, CHUNK:])
        grad[n] = turned.T

    def add_pixel_grad(n):
        first = pl.multiple_of(lax.rem(n, per_step) * CHUNK + CHUNK - PAIR, PAIR)
        cols = pl.ds(first, PAIR)
        high, low = v_high[cols, :], v_low[cols, :]
        v_cat = jnp.concatenate([high, high, low], axis=0)
        for start in range(0, pixels, ROWS):
            rows = pl.ds(start, ROWS)
            high, low = m_high[rows, cols], m_low[rows, cols]
            p_ref[rows, :] += dot(jnp.concatenate([high, low, high], axis=1), v_cat)

    def pair_done(n):
        @pl.when(lax.rem(lax.rem(n, per_step) * CHUNK + CHUNK, PAIR) == 0)
        def _():
            add_pixel_grad(n)

    def serve(t):
        n_sum = t - LAG_SUM

        @pl.when(jnp.logical_and(n_sum >= 0, n_sum < total))
        def _():
            core_copy(n_sum).wait_recv()
            own = grad[n_sum, pl.ds(pl.multiple_of(core * half, half), half), :]
            chip_sum[n_sum, chip] = own + core_in[n_sum]
            for offset in range(1, chips):
                chip_copy(n_sum, offset).start()

        n_new = t - LAG_UPDATE

        @pl.when(jnp.logical_and(n_new >= 0, n_new < total))
        def _():
            for offset in range(1, chips):
                chip_arrival(n_new, offset).wait_recv()
            summed = chip_sum[n_new, 0]
            for index in range(1, chips):
                summed = summed + chip_sum[n_new, index]
            start = lax.rem(n_new, per_step) * CHUNK + core * half
            old = v_all[lax.div(n_new, per_step), pl.ds(pl.multiple_of(start, half), half), :]
            fresh[n_new] = old + scene_rate * summed
            move_copy(n_new).start()

        n_fwd = t - LAG_FORWARD

        @pl.when(n_fwd >= 0)
        def _():
            move_copy(n_fwd).wait_recv()
            forward_copy(n_fwd).start()
            core_copy(n_fwd).wait_send()
            for offset in range(1, chips):
                chip_copy(n_fwd, offset).wait_send()
            move_copy(n_fwd).wait_send()

        @pl.when(n_fwd >= 1)
        def _():
            forward_copy(n_fwd - 1).wait_send()

    def tick(t, carry):
        @pl.when(lax.rem(t, per_step) == 0)
        def _():
            begin_step(lax.div(t, per_step))

        @pl.when(t >= per_step)
        def _():
            forward_arrival(t - per_step).wait_recv()

        work(t)
        core_copy(t).start()
        pair_done(t)
        serve(t)
        return carry

    def late_tick(t, carry):
        serve(t)
        return carry

    begin_step(0)
    work(0)
    pl.semaphore_wait(barrier, len(partners))
    core_copy(0).start()
    lax.fori_loop(1, total, tick, 0)

    for start in range(0, pixels, ROWS):
        rows = pl.ds(start, ROWS)
        u_ref[rows, :] += pixel_rate * p_ref[rows, :]
    store_u = pltpu.make_async_copy(u_ref, pix_out, out_sem.at[0])
    store_u.start()

    lax.fori_loop(total, total + LAG_FORWARD, late_tick, 0)

    def store_v(c):
        cols = pl.ds(pl.multiple_of(c * CHUNK, CHUNK), CHUNK)
        return pltpu.make_async_copy(v_all.at[STEPS, cols], scene_out.at[cols], out_sem.at[1 + c])

    def finish(c, carry):
        forward_arrival((STEPS - 1) * per_step + c).wait_recv()
        store_v(c).start()
        return carry

    lax.fori_loop(0, per_step, finish, 0)
    forward_copy(total - 1).wait_send()

    def stored(c, carry):
        store_v(c).wait()
        return carry

    lax.fori_loop(0, per_step, stored, 0)
    store_u.wait()


def hand_out(first_ref, second_ref, first_out, second_out, sems):
    copies = []
    for source, target in ((first_ref, first_out), (second_ref, second_out)):
        for start in range(0, source.shape[0], ROWS):
            rows = pl.ds(start, ROWS)
            copies.append(pltpu.make_async_copy(source.at[rows], target.at[rows], sems.at[len(copies)]))
    for copy in copies:
        copy.start()
    for copy in copies:
        copy.wait()


def per_device(blk_count, rep_count, pixel_factors, scene_factors, elevations, quality, occupancy):
    pixels, rank = pixel_factors.shape
    acq = scene_factors.shape[0]
    total = STEPS * (acq // CHUNK)
    half = CHUNK // 2
    chips = rep_count // 2
    f32, bf16 = jnp.float32, jnp.bfloat16
    anywhere = pl.BlockSpec(memory_space=pl.ANY)
    dma = pltpu.SemaphoreType.DMA
    new_pixels, new_scene = pl.pallas_call(
        functools.partial(kernel, blk_count, rep_count),
        out_shape=(
            jax.ShapeDtypeStruct((pixels, rank), f32),
            jax.ShapeDtypeStruct((acq, rank), f32),
        ),
        in_specs=[pl.BlockSpec(memory_space=pltpu.SMEM)] + [anywhere] * 4,
        out_specs=(anywhere, anywhere),
        scratch_shapes=[
            pltpu.VMEM(elevations.shape, bf16),
            pltpu.VMEM(quality.shape, bf16),
            pltpu.VMEM((pixels, rank), f32),
            pltpu.VMEM((pixels, rank), f32),
            pltpu.VMEM((2, pixels, rank), bf16),
            pltpu.VMEM((2 * rank, pixels), bf16),
            pltpu.VMEM((STEPS + 1, acq, rank), f32),
            pltpu.VMEM((acq, rank), bf16),
            pltpu.VMEM((acq, rank), bf16),
            pltpu.VMEM((pixels, acq), bf16),
            pltpu.VMEM((pixels, acq), bf16),
            pltpu.VMEM((total, CHUNK, rank), f32),
            pltpu.VMEM((total, half, rank), f32),
            pltpu.VMEM((total, chips, half, rank), f32),
            pltpu.VMEM((total, half, rank), f32),
            dma((2,)),
            dma((1 + acq // CHUNK,)),
            dma((2, STEPS)),
            dma((total,)),
            dma((total,)),
            dma((total, chips)),
            dma((total, chips)),
            dma((total,)),
            dma((total,)),
            dma((total,)),
            dma((total,)),
        ],
        compiler_params=pltpu.CompilerParams(
            collective_id=0, has_side_effects=True, vmem_limit_bytes=VMEM_BYTES
        ),
        cost_estimate=pl.CostEstimate(
            flops=18 * STEPS * pixels * acq * rank, bytes_accessed=12 * 1024 * 1024, transcendentals=0
        ),
    )(occupancy.T, pixel_factors, scene_factors, elevations, quality)
    return pl.pallas_call(
        hand_out,
        out_shape=(
            jax.ShapeDtypeStruct((pixels, rank), f32),
            jax.ShapeDtypeStruct((acq, rank), f32),
        ),
        in_specs=[anywhere] * 2,
        out_specs=(anywhere, anywhere),
        scratch_shapes=[dma(((pixels + acq) // ROWS,))],
        compiler_params=pltpu.CompilerParams(vmem_limit_bytes=VMEM_BYTES),
    )(new_pixels, new_scene)


def solution(mesh):
    in_specs = (
        P(("blk", "rep"), None),
        P("blk", None),
        P(None, ("blk", "rep"), None),
        P(None, ("blk", "rep"), None),
        P(None, ("blk", "rep")),
    )
    out_specs = (P(("blk", "rep"), None), P("blk", None))
    return jax.shard_map(
        functools.partial(per_device, mesh.shape["blk"], mesh.shape["rep"]),
        mesh=mesh, in_specs=in_specs, out_specs=out_specs, check_vma=False,
    )
```

```python
import functools

import jax
import jax.numpy as jnp
from jax import lax
from jax.experimental import pallas as pl
from jax.experimental.pallas import tpu as pltpu
from jax.sharding import PartitionSpec as P

MESH = pl.DeviceIdType.MESH
STEPS = 3
CHUNK = 128
PAIR = 256
ROWS = 256
BAND = 128
VMEM_BYTES = 62 * 1024 * 1024
LAG_SUM = 1
LAG_UPDATE = 3
LAG_FORWARD = 6


def split(value):
    high = value.astype(jnp.bfloat16)
    return high, (value - high.astype(jnp.float32)).astype(jnp.bfloat16)


def dot(left, right):
    return jnp.dot(left, right, preferred_element_type=jnp.float32)


def kernel(
    blk_count, rep_count,
    occ_ref, pix_ref, scene_ref, elev_ref, qual_ref, pix_out, scene_out,
    elev, qual, u_ref, u_parts, ut_parts, v_all, v_high, v_low, m_high, m_low,
    grad, core_in, chip_sum, fresh,
    load_sem, tile_sem, core_send, core_recv, chip_send, chip_recv, move_send, move_recv, fwd_send, fwd_recv,
):
    pixels, rank = pix_ref.shape
    acq = scene_ref.shape[0]
    per_step = acq // CHUNK
    total = STEPS * per_step
    half = CHUNK // 2
    chips = rep_count // 2
    pixel_rate = 8.0 / acq
    scene_rate = 8.0 / (pixels * rep_count)

    group = lax.axis_index("blk")
    rep = lax.axis_index("rep")
    core = lax.rem(rep, 2)
    chip = lax.div(rep, 2)
    other_core = chip * 2 + 1 - core

    def at_blk(shift):
        return lax.rem(group + shift + blk_count, blk_count)

    barrier = pltpu.get_barrier_semaphore()
    partners = [(group, other_core)]
    for offset in range(1, chips):
        partners.append((group, lax.rem(chip + offset, chips) * 2 + core))
    for shift in (-1, 1, STEPS - 1, 1 - STEPS):
        partners.append((at_blk(shift), rep))
    for partner in partners:
        pl.semaphore_signal(barrier, inc=1, device_id=partner, device_id_type=MESH)

    load_u = pltpu.make_async_copy(pix_ref, u_ref, load_sem.at[0])
    load_v = pltpu.make_async_copy(scene_ref, v_all.at[0], load_sem.at[1])
    load_u.start()
    load_v.start()

    def tile_loads(step):
        return (
            pltpu.make_async_copy(elev_ref.at[step], elev.at[step], tile_sem.at[0, step]),
            pltpu.make_async_copy(qual_ref.at[step], qual.at[step], tile_sem.at[1, step]),
        )

    for load in tile_loads(0):
        load.start()

    load_u.wait()
    load_v.wait()

    def core_copy(n):
        return pltpu.make_async_remote_copy(
            src_ref=grad.at[n, pl.ds(pl.multiple_of((1 - core) * half, half), half)],
            dst_ref=core_in.at[n],
            send_sem=core_send.at[n], recv_sem=core_recv.at[n],
            device_id=(group, other_core), device_id_type=MESH,
        )

    def chip_copy(n, offset):
        return pltpu.make_async_remote_copy(
            src_ref=chip_sum.at[n, chip], dst_ref=chip_sum.at[n, chip],
            send_sem=chip_send.at[n, offset - 1], recv_sem=chip_recv.at[n, chip],
            device_id=(group, lax.rem(chip + offset, chips) * 2 + core), device_id_type=MESH,
        )

    def chip_arrival(n, offset):
        sender = lax.rem(chip + offset, chips)
        return pltpu.make_async_remote_copy(
            src_ref=chip_sum.at[n, sender], dst_ref=chip_sum.at[n, sender],
            send_sem=chip_send.at[n, offset - 1], recv_sem=chip_recv.at[n, sender],
            device_id=(group, sender * 2 + core), device_id_type=MESH,
        )

    def place(n, side):
        step = lax.div(n, per_step)
        start = lax.rem(n, per_step) * CHUNK + side * half
        return v_all.at[step + 1, pl.ds(pl.multiple_of(start, half), half)]

    def move_copy(n):
        last = lax.div(lax.div(n, per_step), STEPS - 1)
        return pltpu.make_async_remote_copy(
            src_ref=fresh.at[n], dst_ref=place(n, core),
            send_sem=move_send.at[n], recv_sem=move_recv.at[n],
            device_id=(at_blk(last * STEPS - 1), rep), device_id_type=MESH,
        )

    def forward_copy(n):
        return pltpu.make_async_remote_copy(
            src_ref=place(n, core), dst_ref=place(n, core),
            send_sem=fwd_send.at[n], recv_sem=fwd_recv.at[n],
            device_id=(group, other_core), device_id_type=MESH,
        )

    def forward_arrival(n):
        return pltpu.make_async_remote_copy(
            src_ref=place(n, 1 - core), dst_ref=place(n, 1 - core),
            send_sem=fwd_send.at[n], recv_sem=fwd_recv.at[n],
            device_id=(group, other_core), device_id_type=MESH,
        )

    def begin_step(step):
        for load in tile_loads(step):
            load.wait()

        @pl.when(step + 1 < STEPS)
        def _():
            for load in tile_loads(step + 1):
                load.start()

        for start in range(0, pixels, ROWS):
            rows = pl.ds(start, ROWS)
            u = u_ref[rows, :]
            high, low = split(u)
            u_parts[0, rows, :] = high
            u_parts[1, rows, :] = low
            high, low = split(u.T)
            ut_parts[pl.ds(0, rank), rows] = high
            ut_parts[pl.ds(rank, rank), rows] = low

    def work(n):
        step = lax.div(n, per_step)
        first = pl.multiple_of(lax.rem(n, per_step) * CHUNK, CHUNK)
        cols = pl.ds(first, CHUNK)
        flag = occ_ref[0, step].astype(jnp.float32)
        v = v_all[step, cols, :]
        high, low = split(v)
        v_high[cols, :] = high
        v_low[cols, :] = low
        high, low = split(v.T)
        v_cat = jnp.concatenate([high, low], axis=1)
        for start in range(0, pixels, ROWS):
            rows = pl.ds(start, ROWS)
            by_high = dot(u_parts[0, rows, :], v_cat)
            by_low = dot(u_parts[1, rows, :], v_cat)
            predicted = by_high[:, :CHUNK] + (by_high[:, CHUNK:] + by_low[:, :CHUNK] + by_low[:, CHUNK:])
            weight = qual[step, rows, cols].astype(jnp.float32) * flag
            misfit = weight * (elev[step, rows, cols].astype(jnp.float32) - predicted)
            high, low = split(misfit)
            m_high[rows, cols] = high
            m_low[rows, cols] = low
        parts = dot(ut_parts[...], jnp.concatenate([m_high[:, cols], m_low[:, cols]], axis=1))
        by_high, by_low = parts[:rank], parts[rank:]
        turned = by_high[:, :CHUNK] + (by_high[:, CHUNK:] + by_low[:, :CHUNK] + by_low[:, CHUNK:])
        grad[n] = turned.T

    def add_pixel_grad(n, begin, count):
        first = pl.multiple_of(lax.rem(n, per_step) * CHUNK + CHUNK - PAIR, PAIR)
        cols = pl.ds(first, PAIR)
        high, low = v_high[cols, :], v_low[cols, :]
        v_cat = jnp.concatenate([high, high, low], axis=0)
        for start in range(0, count, BAND):
            rows = pl.ds(pl.multiple_of(begin + start, BAND), BAND)
            high, low = m_high[rows, cols], m_low[rows, cols]
            u_ref[rows, :] += pixel_rate * dot(jnp.concatenate([high, low, high], axis=1), v_cat)

    def serve(t):
        n_sum = t - LAG_SUM

        @pl.when(jnp.logical_and(n_sum >= 0, n_sum < total))
        def _():
            core_copy(n_sum).wait_recv()
            own = grad[n_sum, pl.ds(pl.multiple_of(core * half, half), half), :]
            chip_sum[n_sum, chip] = own + core_in[n_sum]
            for offset in range(1, chips):
                chip_copy(n_sum, offset).start()

        n_new = t - LAG_UPDATE

        @pl.when(jnp.logical_and(n_new >= 0, n_new < total))
        def _():
            for offset in range(1, chips):
                chip_arrival(n_new, offset).wait_recv()
            summed = chip_sum[n_new, 0]
            for index in range(1, chips):
                summed = summed + chip_sum[n_new, index]
            start = lax.rem(n_new, per_step) * CHUNK + core * half
            old = v_all[lax.div(n_new, per_step), pl.ds(pl.multiple_of(start, half), half), :]
            fresh[n_new] = old + scene_rate * summed
            move_copy(n_new).start()

        n_fwd = t - LAG_FORWARD

        @pl.when(n_fwd >= 0)
        def _():
            move_copy(n_fwd).wait_recv()
            forward_copy(n_fwd).start()
            core_copy(n_fwd).wait_send()
            for offset in range(1, chips):
                chip_copy(n_fwd, offset).wait_send()
            move_copy(n_fwd).wait_send()

        @pl.when(n_fwd >= 1)
        def _():
            forward_copy(n_fwd - 1).wait_send()

    pair = PAIR // CHUNK
    part = pixels // pair

    def tick(t, carry):
        place_in_step = lax.rem(t, per_step)

        @pl.when(place_in_step == 0)
        def _():
            add_pixel_grad(t - 1, 0, pixels)
            begin_step(lax.div(t, per_step))

        @pl.when(t >= per_step)
        def _():
            forward_arrival(t - per_step).wait_recv()

        @pl.when(place_in_step < pair)
        def _():
            work(t)

        @pl.when(place_in_step >= pair)
        def _():
            turn = lax.rem(place_in_step, pair)
            work(t)
            add_pixel_grad(t - turn - 1, turn * part, part)

        core_copy(t).start()
        serve(t)
        return carry

    def late_tick(t, carry):
        serve(t)
        return carry

    begin_step(0)
    work(0)
    pl.semaphore_wait(barrier, len(partners))
    core_copy(0).start()
    lax.fori_loop(1, total, tick, 0)

    add_pixel_grad(total - 1, 0, pixels)
    for start in range(0, pixels, ROWS):
        rows = pl.ds(start, ROWS)
        pix_out[rows, :] = u_ref[rows, :]
    lax.fori_loop(total, total + LAG_FORWARD, late_tick, 0)

    def finish(c, carry):
        forward_arrival((STEPS - 1) * per_step + c).wait_recv()
        cols = pl.ds(pl.multiple_of(c * CHUNK, CHUNK), CHUNK)
        scene_out[cols, :] = v_all[STEPS, cols, :]
        return carry

    lax.fori_loop(0, per_step, finish, 0)
    forward_copy(total - 1).wait_send()


def per_device(blk_count, rep_count, pixel_factors, scene_factors, elevations, quality, occupancy):
    pixels, rank = pixel_factors.shape
    acq = scene_factors.shape[0]
    total = STEPS * (acq // CHUNK)
    half = CHUNK // 2
    chips = rep_count // 2
    f32, bf16 = jnp.float32, jnp.bfloat16
    in_vmem = pl.BlockSpec(memory_space=pltpu.VMEM)
    anywhere = pl.BlockSpec(memory_space=pl.ANY)
    dma = pltpu.SemaphoreType.DMA
    return pl.pallas_call(
        functools.partial(kernel, blk_count, rep_count),
        out_shape=(
            pltpu.VMEM((pixels, rank), f32),
            pltpu.VMEM((acq, rank), f32),
        ),
        in_specs=[pl.BlockSpec(memory_space=pltpu.SMEM)] + [anywhere] * 4,
        out_specs=(in_vmem, in_vmem),
        scratch_shapes=[
            pltpu.VMEM(elevations.shape, bf16),
            pltpu.VMEM(quality.shape, bf16),
            pltpu.VMEM((pixels, rank), f32),
            pltpu.VMEM((2, pixels, rank), bf16),
            pltpu.VMEM((2 * rank, pixels), bf16),
            pltpu.VMEM((STEPS + 1, acq, rank), f32),
            pltpu.VMEM((acq, rank), bf16),
            pltpu.VMEM((acq, rank), bf16),
            pltpu.VMEM((pixels, acq), bf16),
            pltpu.VMEM((pixels, acq), bf16),
            pltpu.VMEM((total, CHUNK, rank), f32),
            pltpu.VMEM((total, half, rank), f32),
            pltpu.VMEM((total, chips, half, rank), f32),
            pltpu.VMEM((total, half, rank), f32),
            dma((2,)),
            dma((2, STEPS)),
            dma((total,)),
            dma((total,)),
            dma((total, chips)),
            dma((total, chips)),
            dma((total,)),
            dma((total,)),
            dma((total,)),
            dma((total,)),
        ],
        compiler_params=pltpu.CompilerParams(
            collective_id=0, has_side_effects=True, vmem_limit_bytes=VMEM_BYTES
        ),
        cost_estimate=pl.CostEstimate(
            flops=18 * STEPS * pixels * acq * rank, bytes_accessed=12 * 1024 * 1024, transcendentals=0
        ),
    )(occupancy.T, pixel_factors, scene_factors, elevations, quality)


def solution(mesh):
    in_specs = (
        P(("blk", "rep"), None),
        P("blk", None),
        P(None, ("blk", "rep"), None),
        P(None, ("blk", "rep"), None),
        P(None, ("blk", "rep")),
    )
    out_specs = (P(("blk", "rep"), None), P("blk", None))
    return jax.shard_map(
        functools.partial(per_device, mesh.shape["blk"], mesh.shape["rep"]),
        mesh=mesh, in_specs=in_specs, out_specs=out_specs, check_vma=False,
    )
```

```python
import functools

import jax
import jax.numpy as jnp
from jax import lax
from jax.experimental import pallas as pl
from jax.experimental.pallas import tpu as pltpu
from jax.sharding import PartitionSpec as P

MESH = pl.DeviceIdType.MESH
STEPS = 3
CHUNK = 128
PAIR = 256
ROWS = 256
BAND = 128
VMEM_BYTES = 62 * 1024 * 1024
LAG_SUM = 1
LAG_UPDATE = 3
LAG_FORWARD = 6


def split(value):
    high = value.astype(jnp.bfloat16)
    return high, (value - high.astype(jnp.float32)).astype(jnp.bfloat16)


def dot(left, right):
    return jnp.dot(left, right, preferred_element_type=jnp.float32)


def kernel(
    blk_count, rep_count,
    occ_ref, pix_ref, scene_ref, elev_ref, qual_ref, pix_out, scene_out,
    elev, qual, u_ref, u_parts, ut_parts, v_first, v_all, v_high, v_low, m_high, m_low,
    grad, core_in, chip_sum, fresh,
    load_sem, first_sem, tile_sem, send_sem, core_recv, chip_recv, move_recv, fwd_recv,
):
    pixels, rank = pix_ref.shape
    acq = scene_ref.shape[0]
    per_step = acq // CHUNK
    total = STEPS * per_step
    half = rank // 2
    chips = rep_count // 2
    pixel_rate = 8.0 / acq
    scene_rate = 8.0 / (pixels * rep_count)

    group = lax.axis_index("blk")
    rep = lax.axis_index("rep")
    core = lax.rem(rep, 2)
    chip = lax.div(rep, 2)
    other_core = chip * 2 + 1 - core

    def at_blk(shift):
        return lax.rem(group + shift + blk_count, blk_count)

    barrier = pltpu.get_barrier_semaphore()
    partners = [(group, other_core)]
    for offset in range(1, chips):
        partners.append((group, lax.rem(chip + offset, chips) * 2 + core))
    for shift in (-1, 1, STEPS - 1, 1 - STEPS):
        partners.append((at_blk(shift), rep))
    for partner in partners:
        pl.semaphore_signal(barrier, inc=1, device_id=partner, device_id_type=MESH)

    load_u = pltpu.make_async_copy(pix_ref, u_ref, load_sem.at[0])
    load_u.start()

    def first_loads(c):
        cols = pl.ds(pl.multiple_of(c * CHUNK, CHUNK), CHUNK)
        return (
            pltpu.make_async_copy(scene_ref.at[cols], v_first.at[cols], first_sem.at[0, c]),
            pltpu.make_async_copy(elev_ref.at[0, :, cols], elev.at[0, :, cols], first_sem.at[1, c]),
            pltpu.make_async_copy(qual_ref.at[0, :, cols], qual.at[0, :, cols], first_sem.at[2, c]),
        )

    for c in range(per_step):
        for load in first_loads(c):
            load.start()

    def tile_loads(step):
        return (
            pltpu.make_async_copy(elev_ref.at[step], elev.at[step], tile_sem.at[0, step]),
            pltpu.make_async_copy(qual_ref.at[step], qual.at[step], tile_sem.at[1, step]),
        )


    load_u.wait()

    def core_copy(n):
        return pltpu.make_async_remote_copy(
            src_ref=grad.at[n, pl.ds(pl.multiple_of((1 - core) * half, half), half)],
            dst_ref=core_in.at[n],
            send_sem=send_sem.at[0], recv_sem=core_recv.at[n],
            device_id=(group, other_core), device_id_type=MESH,
        )

    def chip_copy(n, offset):
        return pltpu.make_async_remote_copy(
            src_ref=chip_sum.at[n, chip], dst_ref=chip_sum.at[n, chip],
            send_sem=send_sem.at[2 + offset], recv_sem=chip_recv.at[n, chip],
            device_id=(group, lax.rem(chip + offset, chips) * 2 + core), device_id_type=MESH,
        )

    def chip_arrival(n, offset):
        sender = lax.rem(chip + offset, chips)
        return pltpu.make_async_remote_copy(
            src_ref=chip_sum.at[n, sender], dst_ref=chip_sum.at[n, sender],
            send_sem=send_sem.at[2 + offset], recv_sem=chip_recv.at[n, sender],
            device_id=(group, sender * 2 + core), device_id_type=MESH,
        )

    def place(n, side):
        step = lax.div(n, per_step)
        return v_all.at[step + 1, lax.rem(n, per_step), pl.ds(pl.multiple_of(side * half, half), half)]

    def move_copy(n):
        last = lax.div(lax.div(n, per_step), STEPS - 1)
        return pltpu.make_async_remote_copy(
            src_ref=fresh.at[n], dst_ref=place(n, core),
            send_sem=send_sem.at[1], recv_sem=move_recv.at[n],
            device_id=(at_blk(last * STEPS - 1), rep), device_id_type=MESH,
        )

    def forward_copy(n):
        return pltpu.make_async_remote_copy(
            src_ref=place(n, core), dst_ref=place(n, core),
            send_sem=send_sem.at[2], recv_sem=fwd_recv.at[n],
            device_id=(group, other_core), device_id_type=MESH,
        )

    def forward_arrival(n):
        return pltpu.make_async_remote_copy(
            src_ref=place(n, 1 - core), dst_ref=place(n, 1 - core),
            send_sem=send_sem.at[2], recv_sem=fwd_recv.at[n],
            device_id=(group, other_core), device_id_type=MESH,
        )

    def begin_step(step):
        @pl.when(step > 0)
        def _():
            for load in tile_loads(step):
                load.wait()

        @pl.when(step + 1 < STEPS)
        def _():
            for load in tile_loads(step + 1):
                load.start()

        for start in range(0, pixels, ROWS):
            rows = pl.ds(start, ROWS)
            u = u_ref[rows, :]
            high, low = split(u)
            u_parts[0, rows, :] = high
            u_parts[1, rows, :] = low
            high, low = split(u.T)
            ut_parts[pl.ds(0, rank), rows] = high
            ut_parts[pl.ds(rank, rank), rows] = low

    def work(n):
        step = lax.div(n, per_step)
        first = pl.multiple_of(lax.rem(n, per_step) * CHUNK, CHUNK)
        cols = pl.ds(first, CHUNK)
        flag = occ_ref[0, step].astype(jnp.float32)
        v = v_all[step, lax.rem(n, per_step)]
        high, low = split(v.T)
        v_high[cols, :] = high
        v_low[cols, :] = low
        high, low = split(v)
        v_cat = jnp.concatenate([high, low], axis=1)
        for start in range(0, pixels, ROWS):
            rows = pl.ds(start, ROWS)
            by_high = dot(u_parts[0, rows, :], v_cat)
            by_low = dot(u_parts[1, rows, :], v_cat)
            predicted = by_high[:, :CHUNK] + (by_high[:, CHUNK:] + by_low[:, :CHUNK] + by_low[:, CHUNK:])
            weight = qual[step, rows, cols].astype(jnp.float32) * flag
            misfit = weight * (elev[step, rows, cols].astype(jnp.float32) - predicted)
            high, low = split(misfit)
            m_high[rows, cols] = high
            m_low[rows, cols] = low
        parts = dot(ut_parts[...], jnp.concatenate([m_high[:, cols], m_low[:, cols]], axis=1))
        by_high, by_low = parts[:rank], parts[rank:]
        grad[n] = by_high[:, :CHUNK] + (by_high[:, CHUNK:] + by_low[:, :CHUNK] + by_low[:, CHUNK:])

    def add_pixel_grad(n, begin, count):
        first = pl.multiple_of(lax.rem(n, per_step) * CHUNK + CHUNK - PAIR, PAIR)
        cols = pl.ds(first, PAIR)
        high, low = v_high[cols, :], v_low[cols, :]
        v_cat = jnp.concatenate([high, high, low], axis=0)
        for start in range(0, count, BAND):
            rows = pl.ds(pl.multiple_of(begin + start, BAND), BAND)
            high, low = m_high[rows, cols], m_low[rows, cols]
            u_ref[rows, :] += pixel_rate * dot(jnp.concatenate([high, low, high], axis=1), v_cat)

    def serve(t):
        n_sum = t - LAG_SUM

        @pl.when(jnp.logical_and(n_sum >= 0, n_sum < total))
        def _():
            core_copy(n_sum).wait_recv()
            own = grad[n_sum, pl.ds(pl.multiple_of(core * half, half), half), :]
            chip_sum[n_sum, chip] = own + core_in[n_sum]
            for offset in range(1, chips):
                chip_copy(n_sum, offset).start()

        n_new = t - LAG_UPDATE

        @pl.when(jnp.logical_and(n_new >= 0, n_new < total))
        def _():
            for offset in range(1, chips):
                chip_arrival(n_new, offset).wait_recv()
            summed = chip_sum[n_new, 0]
            for index in range(1, chips):
                summed = summed + chip_sum[n_new, index]
            old = v_all[lax.div(n_new, per_step), lax.rem(n_new, per_step), pl.ds(pl.multiple_of(core * half, half), half)]
            fresh[n_new] = old + scene_rate * summed
            move_copy(n_new).start()

        n_fwd = t - LAG_FORWARD

        @pl.when(n_fwd >= 0)
        def _():
            move_copy(n_fwd).wait_recv()
            forward_copy(n_fwd).start()

    pair = PAIR // CHUNK
    part = pixels // pair

    def take_first(c):
        for load in first_loads(c):
            load.wait()
        v_all[0, c] = v_first[pl.ds(pl.multiple_of(c * CHUNK, CHUNK), CHUNK), :].T

    def tick(t, carry):
        place_in_step = lax.rem(t, per_step)

        @pl.when(place_in_step == 0)
        def _():
            add_pixel_grad(t - 1, 0, pixels)
            begin_step(lax.div(t, per_step))

        @pl.when(t < per_step)
        def _():
            take_first(t)

        @pl.when(t >= per_step)
        def _():
            forward_arrival(t - per_step).wait_recv()

        @pl.when(place_in_step < pair)
        def _():
            work(t)

        @pl.when(place_in_step >= pair)
        def _():
            turn = lax.rem(place_in_step, pair)
            work(t)
            add_pixel_grad(t - turn - 1, turn * part, part)

        core_copy(t).start()
        serve(t)
        return carry

    def late_tick(t, carry):
        serve(t)
        return carry

    begin_step(0)
    take_first(0)
    work(0)
    pl.semaphore_wait(barrier, len(partners))
    core_copy(0).start()
    lax.fori_loop(1, total, tick, 0)

    add_pixel_grad(total - 1, 0, pixels)
    for start in range(0, pixels, ROWS):
        rows = pl.ds(start, ROWS)
        pix_out[rows, :] = u_ref[rows, :]
    lax.fori_loop(total, total + LAG_FORWARD, late_tick, 0)

    def finish(c, carry):
        forward_arrival((STEPS - 1) * per_step + c).wait_recv()
        cols = pl.ds(pl.multiple_of(c * CHUNK, CHUNK), CHUNK)
        scene_out[cols, :] = v_all[STEPS, c].T
        return carry

    lax.fori_loop(0, per_step, finish, 0)
    whole = [core_in, fresh, fresh] + [core_in] * (chips - 1)
    for index, like in enumerate(whole):
        pltpu.make_async_copy(like, like, send_sem.at[index]).wait()


def per_device(blk_count, rep_count, pixel_factors, scene_factors, elevations, quality, occupancy):
    pixels, rank = pixel_factors.shape
    acq = scene_factors.shape[0]
    total = STEPS * (acq // CHUNK)
    half = rank // 2
    chips = rep_count // 2
    f32, bf16 = jnp.float32, jnp.bfloat16
    in_vmem = pl.BlockSpec(memory_space=pltpu.VMEM)
    anywhere = pl.BlockSpec(memory_space=pl.ANY)
    dma = pltpu.SemaphoreType.DMA
    return pl.pallas_call(
        functools.partial(kernel, blk_count, rep_count),
        out_shape=(
            pltpu.VMEM((pixels, rank), f32),
            pltpu.VMEM((acq, rank), f32),
        ),
        in_specs=[pl.BlockSpec(memory_space=pltpu.SMEM)] + [anywhere] * 4,
        out_specs=(in_vmem, in_vmem),
        scratch_shapes=[
            pltpu.VMEM(elevations.shape, bf16),
            pltpu.VMEM(quality.shape, bf16),
            pltpu.VMEM((pixels, rank), f32),
            pltpu.VMEM((2, pixels, rank), bf16),
            pltpu.VMEM((2 * rank, pixels), bf16),
            pltpu.VMEM((acq, rank), f32),
            pltpu.VMEM((STEPS + 1, acq // CHUNK, rank, CHUNK), f32),
            pltpu.VMEM((acq, rank), bf16),
            pltpu.VMEM((acq, rank), bf16),
            pltpu.VMEM((pixels, acq), bf16),
            pltpu.VMEM((pixels, acq), bf16),
            pltpu.VMEM((total, rank, CHUNK), f32),
            pltpu.VMEM((total, half, CHUNK), f32),
            pltpu.VMEM((total, chips, half, CHUNK), f32),
            pltpu.VMEM((total, half, CHUNK), f32),
            dma((1,)),
            dma((3, acq // CHUNK)),
            dma((2, STEPS)),
            dma((2 + chips,)),
            dma((total,)),
            dma((total, chips)),
            dma((total,)),
            dma((total,)),
        ],
        compiler_params=pltpu.CompilerParams(
            collective_id=0, has_side_effects=True, vmem_limit_bytes=VMEM_BYTES
        ),
        cost_estimate=pl.CostEstimate(
            flops=18 * STEPS * pixels * acq * rank, bytes_accessed=12 * 1024 * 1024, transcendentals=0
        ),
    )(occupancy.T, pixel_factors, scene_factors, elevations, quality)


def solution(mesh):
    in_specs = (
        P(("blk", "rep"), None),
        P("blk", None),
        P(None, ("blk", "rep"), None),
        P(None, ("blk", "rep"), None),
        P(None, ("blk", "rep")),
    )
    out_specs = (P(("blk", "rep"), None), P("blk", None))
    return jax.shard_map(
        functools.partial(per_device, mesh.shape["blk"], mesh.shape["rep"]),
        mesh=mesh, in_specs=in_specs, out_specs=out_specs, check_vma=False,
    )
```

```python
import functools

import jax
import jax.numpy as jnp
from jax import lax
from jax.experimental import pallas as pl
from jax.experimental.pallas import tpu as pltpu
from jax.sharding import PartitionSpec as P

MESH = pl.DeviceIdType.MESH
STEPS = 3
CHUNK = 128
PAIR = 256
ROWS = 256
BAND = 128
VMEM_BYTES = 62 * 1024 * 1024
LAG_UPDATE = 3
LAG_FORWARD = 6


def split(value):
    high = value.astype(jnp.bfloat16)
    return high, (value - high.astype(jnp.float32)).astype(jnp.bfloat16)


def dot(left, right):
    return jnp.dot(left, right, preferred_element_type=jnp.float32)


def kernel(
    blk_count, rep_count,
    occ_ref, pix_ref, scene_ref, elev_ref, qual_ref, pix_out, scene_out,
    elev, qual, u_ref, u_parts, ut_parts, v_first, v_all, v_high, v_low, m_high, m_low,
    grad, core_in, chip_sum, fresh,
    load_sem, first_sem, tile_sem, send_sem, core_recv, chip_recv, move_recv, fwd_recv,
):
    pixels, rank = pix_ref.shape
    acq = scene_ref.shape[0]
    per_step = acq // CHUNK
    total = STEPS * per_step
    half = rank // 2
    chips = rep_count // 2
    pixel_rate = 8.0 / acq
    scene_rate = 8.0 / (pixels * rep_count)

    group = lax.axis_index("blk")
    rep = lax.axis_index("rep")
    core = lax.rem(rep, 2)
    chip = lax.div(rep, 2)
    other_core = chip * 2 + 1 - core

    def at_blk(shift):
        return lax.rem(group + shift + blk_count, blk_count)

    barrier = pltpu.get_barrier_semaphore()
    partners = [(group, other_core)]
    for offset in range(1, chips):
        partners.append((group, lax.rem(chip + offset, chips) * 2 + core))
    for shift in (-1, 1, STEPS - 1, 1 - STEPS):
        partners.append((at_blk(shift), rep))
    for partner in partners:
        pl.semaphore_signal(barrier, inc=1, device_id=partner, device_id_type=MESH)

    load_u = pltpu.make_async_copy(pix_ref, u_ref, load_sem.at[0])
    load_u.start()

    def first_loads(c):
        cols = pl.ds(pl.multiple_of(c * CHUNK, CHUNK), CHUNK)
        return (
            pltpu.make_async_copy(scene_ref.at[cols], v_first.at[cols], first_sem.at[0, c]),
            pltpu.make_async_copy(elev_ref.at[0, :, cols], elev.at[0, :, cols], first_sem.at[1, c]),
            pltpu.make_async_copy(qual_ref.at[0, :, cols], qual.at[0, :, cols], first_sem.at[2, c]),
        )

    for c in range(per_step):
        for load in first_loads(c):
            load.start()

    def tile_loads(step):
        return (
            pltpu.make_async_copy(elev_ref.at[step], elev.at[step], tile_sem.at[0, step]),
            pltpu.make_async_copy(qual_ref.at[step], qual.at[step], tile_sem.at[1, step]),
        )


    load_u.wait()

    def core_copy(n):
        return pltpu.make_async_remote_copy(
            src_ref=grad.at[n, pl.ds(pl.multiple_of((1 - core) * half, half), half)],
            dst_ref=core_in.at[n],
            send_sem=send_sem.at[0], recv_sem=core_recv.at[n],
            device_id=(group, other_core), device_id_type=MESH,
        )

    def chip_copy(n, offset):
        return pltpu.make_async_remote_copy(
            src_ref=chip_sum.at[n, chip], dst_ref=chip_sum.at[n, chip],
            send_sem=send_sem.at[2 + offset], recv_sem=chip_recv.at[n, chip],
            device_id=(group, lax.rem(chip + offset, chips) * 2 + core), device_id_type=MESH,
        )

    def chip_arrival(n, offset):
        sender = lax.rem(chip + offset, chips)
        return pltpu.make_async_remote_copy(
            src_ref=chip_sum.at[n, sender], dst_ref=chip_sum.at[n, sender],
            send_sem=send_sem.at[2 + offset], recv_sem=chip_recv.at[n, sender],
            device_id=(group, sender * 2 + core), device_id_type=MESH,
        )

    def place(n, side):
        step = lax.div(n, per_step)
        return v_all.at[step + 1, lax.rem(n, per_step), pl.ds(pl.multiple_of(side * half, half), half)]

    def move_copy(n):
        last = lax.div(lax.div(n, per_step), STEPS - 1)
        return pltpu.make_async_remote_copy(
            src_ref=fresh.at[n], dst_ref=place(n, core),
            send_sem=send_sem.at[1], recv_sem=move_recv.at[n],
            device_id=(at_blk(last * STEPS - 1), rep), device_id_type=MESH,
        )

    def forward_copy(n):
        return pltpu.make_async_remote_copy(
            src_ref=place(n, core), dst_ref=place(n, core),
            send_sem=send_sem.at[2], recv_sem=fwd_recv.at[n],
            device_id=(group, other_core), device_id_type=MESH,
        )

    def forward_arrival(n):
        return pltpu.make_async_remote_copy(
            src_ref=place(n, 1 - core), dst_ref=place(n, 1 - core),
            send_sem=send_sem.at[2], recv_sem=fwd_recv.at[n],
            device_id=(group, other_core), device_id_type=MESH,
        )

    def begin_step(step):
        @pl.when(step > 0)
        def _():
            for load in tile_loads(step):
                load.wait()

        @pl.when(step + 1 < STEPS)
        def _():
            for load in tile_loads(step + 1):
                load.start()

        for start in range(0, pixels, ROWS):
            rows = pl.ds(start, ROWS)
            u = u_ref[rows, :]
            high, low = split(u)
            u_parts[0, rows, :] = high
            u_parts[1, rows, :] = low
            high, low = split(u.T)
            ut_parts[pl.ds(0, rank), rows] = high
            ut_parts[pl.ds(rank, rank), rows] = low

    def misfits(n):
        step = lax.div(n, per_step)
        first = pl.multiple_of(lax.rem(n, per_step) * CHUNK, CHUNK)
        cols = pl.ds(first, CHUNK)
        flag = occ_ref[0, step].astype(jnp.float32)
        v = v_all[step, lax.rem(n, per_step)]
        high, low = split(v.T)
        v_high[cols, :] = high
        v_low[cols, :] = low
        high, low = split(v)
        v_cat = jnp.concatenate([high, low], axis=1)
        for start in range(0, pixels, ROWS):
            rows = pl.ds(start, ROWS)
            by_high = dot(u_parts[0, rows, :], v_cat)
            by_low = dot(u_parts[1, rows, :], v_cat)
            predicted = by_high[:, :CHUNK] + (by_high[:, CHUNK:] + by_low[:, :CHUNK] + by_low[:, CHUNK:])
            weight = qual[step, rows, cols].astype(jnp.float32) * flag
            misfit = weight * (elev[step, rows, cols].astype(jnp.float32) - predicted)
            high, low = split(misfit)
            m_high[rows, cols] = high
            m_low[rows, cols] = low

    def scene_grad(n):
        cols = pl.ds(pl.multiple_of(lax.rem(n, per_step) * CHUNK, CHUNK), CHUNK)
        parts = dot(ut_parts[...], jnp.concatenate([m_high[:, cols], m_low[:, cols]], axis=1))
        by_high, by_low = parts[:rank], parts[rank:]
        grad[n] = by_high[:, :CHUNK] + (by_high[:, CHUNK:] + by_low[:, :CHUNK] + by_low[:, CHUNK:])

    def add_pixel_grad(n, begin, count):
        first = pl.multiple_of(lax.rem(n, per_step) * CHUNK + CHUNK - PAIR, PAIR)
        cols = pl.ds(first, PAIR)
        high, low = v_high[cols, :], v_low[cols, :]
        v_cat = jnp.concatenate([high, high, low], axis=0)
        for start in range(0, count, BAND):
            rows = pl.ds(pl.multiple_of(begin + start, BAND), BAND)
            high, low = m_high[rows, cols], m_low[rows, cols]
            u_ref[rows, :] += pixel_rate * dot(jnp.concatenate([high, low, high], axis=1), v_cat)

    def stage(n, body):
        @pl.when(jnp.logical_and(n >= 0, n < total))
        def _():
            body(n)

    def add_cores(n):
        core_copy(n).wait_recv()
        own = grad[n, pl.ds(pl.multiple_of(core * half, half), half), :]
        chip_sum[n, chip] = own + core_in[n]
        for offset in range(1, chips):
            chip_copy(n, offset).start()

    def update(n):
        for offset in range(1, chips):
            chip_arrival(n, offset).wait_recv()
        summed = chip_sum[n, 0]
        for index in range(1, chips):
            summed = summed + chip_sum[n, index]
        old = v_all[lax.div(n, per_step), lax.rem(n, per_step), pl.ds(pl.multiple_of(core * half, half), half)]
        fresh[n] = old + scene_rate * summed
        move_copy(n).start()

    def forward(n):
        move_copy(n).wait_recv()
        forward_copy(n).start()

    pair = PAIR // CHUNK
    part = pixels // pair

    def take_first(c):
        for load in first_loads(c):
            load.wait()
        v_all[0, c] = v_first[pl.ds(pl.multiple_of(c * CHUNK, CHUNK), CHUNK), :].T

    def tick(t, carry):
        place_in_step = lax.rem(t, per_step)

        @pl.when(place_in_step == 0)
        def _():
            add_pixel_grad(t - 1, 0, pixels)
            add_cores(t - 1)
            begin_step(lax.div(t, per_step))

        @pl.when(t < per_step)
        def _():
            take_first(t)

        @pl.when(t >= per_step)
        def _():
            forward_arrival(t - per_step).wait_recv()

        @pl.when(place_in_step < pair)
        def _():
            misfits(t)

        @pl.when(place_in_step >= pair)
        def _():
            turn = lax.rem(place_in_step, pair)
            misfits(t)
            add_pixel_grad(t - turn - 1, turn * part, part)

        @pl.when(place_in_step != 0)
        def _():
            add_cores(t - 1)

        stage(t - LAG_FORWARD, forward)
        scene_grad(t)
        core_copy(t).start()
        stage(t - LAG_UPDATE, update)
        return carry

    def late_tick(t, carry):
        stage(t - LAG_UPDATE, update)
        stage(t - LAG_FORWARD, forward)
        return carry

    begin_step(0)
    take_first(0)
    misfits(0)
    scene_grad(0)
    pl.semaphore_wait(barrier, len(partners))
    core_copy(0).start()
    lax.fori_loop(1, total, tick, 0)

    add_pixel_grad(total - 1, 0, pixels)
    add_cores(total - 1)
    for start in range(0, pixels, ROWS):
        rows = pl.ds(start, ROWS)
        pix_out[rows, :] = u_ref[rows, :]
    lax.fori_loop(total, total + LAG_FORWARD, late_tick, 0)

    def finish(c, carry):
        forward_arrival((STEPS - 1) * per_step + c).wait_recv()
        cols = pl.ds(pl.multiple_of(c * CHUNK, CHUNK), CHUNK)
        scene_out[cols, :] = v_all[STEPS, c].T
        return carry

    lax.fori_loop(0, per_step, finish, 0)
    whole = [core_in, fresh, fresh] + [core_in] * (chips - 1)
    for index, like in enumerate(whole):
        pltpu.make_async_copy(like, like, send_sem.at[index]).wait()


def per_device(blk_count, rep_count, pixel_factors, scene_factors, elevations, quality, occupancy):
    pixels, rank = pixel_factors.shape
    acq = scene_factors.shape[0]
    total = STEPS * (acq // CHUNK)
    half = rank // 2
    chips = rep_count // 2
    f32, bf16 = jnp.float32, jnp.bfloat16
    in_vmem = pl.BlockSpec(memory_space=pltpu.VMEM)
    anywhere = pl.BlockSpec(memory_space=pl.ANY)
    dma = pltpu.SemaphoreType.DMA
    return pl.pallas_call(
        functools.partial(kernel, blk_count, rep_count),
        out_shape=(
            pltpu.VMEM((pixels, rank), f32),
            pltpu.VMEM((acq, rank), f32),
        ),
        in_specs=[pl.BlockSpec(memory_space=pltpu.SMEM)] + [anywhere] * 4,
        out_specs=(in_vmem, in_vmem),
        scratch_shapes=[
            pltpu.VMEM(elevations.shape, bf16),
            pltpu.VMEM(quality.shape, bf16),
            pltpu.VMEM((pixels, rank), f32),
            pltpu.VMEM((2, pixels, rank), bf16),
            pltpu.VMEM((2 * rank, pixels), bf16),
            pltpu.VMEM((acq, rank), f32),
            pltpu.VMEM((STEPS + 1, acq // CHUNK, rank, CHUNK), f32),
            pltpu.VMEM((acq, rank), bf16),
            pltpu.VMEM((acq, rank), bf16),
            pltpu.VMEM((pixels, acq), bf16),
            pltpu.VMEM((pixels, acq), bf16),
            pltpu.VMEM((total, rank, CHUNK), f32),
            pltpu.VMEM((total, half, CHUNK), f32),
            pltpu.VMEM((total, chips, half, CHUNK), f32),
            pltpu.VMEM((total, half, CHUNK), f32),
            dma((1,)),
            dma((3, acq // CHUNK)),
            dma((2, STEPS)),
            dma((2 + chips,)),
            dma((total,)),
            dma((total, chips)),
            dma((total,)),
            dma((total,)),
        ],
        compiler_params=pltpu.CompilerParams(
            collective_id=0, has_side_effects=True, vmem_limit_bytes=VMEM_BYTES
        ),
        cost_estimate=pl.CostEstimate(
            flops=18 * STEPS * pixels * acq * rank, bytes_accessed=12 * 1024 * 1024, transcendentals=0
        ),
    )(occupancy.T, pixel_factors, scene_factors, elevations, quality)


def solution(mesh):
    in_specs = (
        P(("blk", "rep"), None),
        P("blk", None),
        P(None, ("blk", "rep"), None),
        P(None, ("blk", "rep"), None),
        P(None, ("blk", "rep")),
    )
    out_specs = (P(("blk", "rep"), None), P("blk", None))
    return jax.shard_map(
        functools.partial(per_device, mesh.shape["blk"], mesh.shape["rep"]),
        mesh=mesh, in_specs=in_specs, out_specs=out_specs, check_vma=False,
    )
```

```python
import functools

import jax
import jax.numpy as jnp
from jax import lax
from jax.experimental import pallas as pl
from jax.experimental.pallas import tpu as pltpu
from jax.sharding import PartitionSpec as P

MESH = pl.DeviceIdType.MESH
STEPS = 3
CHUNK = 128
PAIR = 256
ROWS = 256
VMEM_BYTES = 62 * 1024 * 1024
LAG_UPDATE = 3
LAG_FORWARD = 6


def split(value):
    high = value.astype(jnp.bfloat16)
    return high, (value - high.astype(jnp.float32)).astype(jnp.bfloat16)


def dot(left, right):
    return jnp.dot(left, right, preferred_element_type=jnp.float32)


def kernel(
    blk_count, rep_count,
    occ_ref, pix_ref, scene_ref, elev_ref, qual_ref, pix_out, scene_out,
    elev, qual, u_ref, u_parts, ut_parts, v_first, v_all, v_high, v_low, m_high, m_low,
    grad, core_in, chip_sum, fresh,
    load_sem, first_sem, tile_sem, send_sem, core_recv, chip_recv, move_recv, fwd_recv,
):
    pixels, rank = pix_ref.shape
    acq = scene_ref.shape[0]
    per_step = acq // CHUNK
    total = STEPS * per_step
    half = rank // 2
    chips = rep_count // 2
    pixel_rate = 8.0 / acq
    scene_rate = 8.0 / (pixels * rep_count)

    group = lax.axis_index("blk")
    rep = lax.axis_index("rep")
    core = lax.rem(rep, 2)
    chip = lax.div(rep, 2)
    other_core = chip * 2 + 1 - core

    def at_blk(shift):
        return lax.rem(group + shift + blk_count, blk_count)

    barrier = pltpu.get_barrier_semaphore()
    partners = [(group, other_core)]
    for offset in range(1, chips):
        partners.append((group, lax.rem(chip + offset, chips) * 2 + core))
    for shift in (-1, 1, STEPS - 1, 1 - STEPS):
        partners.append((at_blk(shift), rep))
    for partner in partners:
        pl.semaphore_signal(barrier, inc=1, device_id=partner, device_id_type=MESH)

    load_u = pltpu.make_async_copy(pix_ref, u_ref, load_sem.at[0])
    load_u.start()

    def first_loads(c):
        cols = pl.ds(pl.multiple_of(c * CHUNK, CHUNK), CHUNK)
        return (
            pltpu.make_async_copy(scene_ref.at[cols], v_first.at[cols], first_sem.at[0, c]),
            pltpu.make_async_copy(elev_ref.at[0, :, cols], elev.at[0, :, cols], first_sem.at[1, c]),
            pltpu.make_async_copy(qual_ref.at[0, :, cols], qual.at[0, :, cols], first_sem.at[2, c]),
        )

    for c in range(per_step):
        for load in first_loads(c):
            load.start()

    def tile_loads(step):
        return (
            pltpu.make_async_copy(elev_ref.at[step], elev.at[step], tile_sem.at[0, step]),
            pltpu.make_async_copy(qual_ref.at[step], qual.at[step], tile_sem.at[1, step]),
        )


    load_u.wait()

    def core_copy(n):
        return pltpu.make_async_remote_copy(
            src_ref=grad.at[n, pl.ds(pl.multiple_of((1 - core) * half, half), half)],
            dst_ref=core_in.at[n],
            send_sem=send_sem.at[0], recv_sem=core_recv.at[n],
            device_id=(group, other_core), device_id_type=MESH,
        )

    def chip_copy(n, offset):
        return pltpu.make_async_remote_copy(
            src_ref=chip_sum.at[n, chip], dst_ref=chip_sum.at[n, chip],
            send_sem=send_sem.at[2 + offset], recv_sem=chip_recv.at[n, chip],
            device_id=(group, lax.rem(chip + offset, chips) * 2 + core), device_id_type=MESH,
        )

    def chip_arrival(n, offset):
        sender = lax.rem(chip + offset, chips)
        return pltpu.make_async_remote_copy(
            src_ref=chip_sum.at[n, sender], dst_ref=chip_sum.at[n, sender],
            send_sem=send_sem.at[2 + offset], recv_sem=chip_recv.at[n, sender],
            device_id=(group, sender * 2 + core), device_id_type=MESH,
        )

    def place(n, side):
        step = lax.div(n, per_step)
        return v_all.at[step + 1, lax.rem(n, per_step), pl.ds(pl.multiple_of(side * half, half), half)]

    def move_copy(n):
        last = lax.div(lax.div(n, per_step), STEPS - 1)
        return pltpu.make_async_remote_copy(
            src_ref=fresh.at[n], dst_ref=place(n, core),
            send_sem=send_sem.at[1], recv_sem=move_recv.at[n],
            device_id=(at_blk(last * STEPS - 1), rep), device_id_type=MESH,
        )

    def forward_copy(n):
        return pltpu.make_async_remote_copy(
            src_ref=place(n, core), dst_ref=place(n, core),
            send_sem=send_sem.at[2], recv_sem=fwd_recv.at[n],
            device_id=(group, other_core), device_id_type=MESH,
        )

    def forward_arrival(n):
        return pltpu.make_async_remote_copy(
            src_ref=place(n, 1 - core), dst_ref=place(n, 1 - core),
            send_sem=send_sem.at[2], recv_sem=fwd_recv.at[n],
            device_id=(group, other_core), device_id_type=MESH,
        )

    def begin_step(step):
        @pl.when(step > 0)
        def _():
            for load in tile_loads(step):
                load.wait()

        @pl.when(step + 1 < STEPS)
        def _():
            for load in tile_loads(step + 1):
                load.start()

        for start in range(0, pixels, ROWS):
            rows = pl.ds(start, ROWS)
            u = u_ref[rows, :]
            high, low = split(u)
            u_parts[rows, :] = high
            u_parts[pl.ds(pixels + start, ROWS), :] = low
            high, low = split(u.T)
            ut_parts[pl.ds(0, rank), rows] = high
            ut_parts[pl.ds(rank, rank), rows] = low

    pair = PAIR // CHUNK
    part = pixels // pair

    def misfits(n):
        step = lax.div(n, per_step)
        first = pl.multiple_of(lax.rem(n, per_step) * CHUNK, CHUNK)
        cols = pl.ds(first, CHUNK)
        flag = occ_ref[0, step].astype(jnp.float32)
        v = v_all[step, lax.rem(n, per_step)]
        high, low = split(v.T)
        v_high[cols, :] = high
        v_low[cols, :] = low
        high, low = split(v)
        v_cat = jnp.concatenate([high, low], axis=1)
        products = dot(u_parts[...], v_cat)
        for start in range(0, pixels, ROWS):
            rows = pl.ds(start, ROWS)
            by_high = products[start : start + ROWS]
            by_low = products[pixels + start : pixels + start + ROWS]
            predicted = by_high[:, :CHUNK] + (by_high[:, CHUNK:] + by_low[:, :CHUNK] + by_low[:, CHUNK:])
            weight = qual[step, rows, cols].astype(jnp.float32) * flag
            misfit = weight * (elev[step, rows, cols].astype(jnp.float32) - predicted)
            high, low = split(misfit)
            m_high[rows, cols] = high
            m_low[rows, cols] = low

    def scene_grad(n):
        cols = pl.ds(pl.multiple_of(lax.rem(n, per_step) * CHUNK, CHUNK), CHUNK)
        parts = dot(ut_parts[...], jnp.concatenate([m_high[:, cols], m_low[:, cols]], axis=1))
        by_high, by_low = parts[:rank], parts[rank:]
        grad[n] = by_high[:, :CHUNK] + (by_high[:, CHUNK:] + by_low[:, :CHUNK] + by_low[:, CHUNK:])

    def add_pixel_grad(n, begin, count):
        first = pl.multiple_of(lax.rem(n, per_step) * CHUNK + CHUNK - PAIR, PAIR)
        cols = pl.ds(first, PAIR)
        high, low = v_high[cols, :], v_low[cols, :]
        v_cat = jnp.concatenate([high, high, low], axis=0)
        rows = pl.ds(pl.multiple_of(begin, part), count)
        high, low = m_high[rows, cols], m_low[rows, cols]
        u_ref[rows, :] += pixel_rate * dot(jnp.concatenate([high, low, high], axis=1), v_cat)

    def stage(n, body):
        @pl.when(jnp.logical_and(n >= 0, n < total))
        def _():
            body(n)

    def add_cores(n):
        core_copy(n).wait_recv()
        own = grad[n, pl.ds(pl.multiple_of(core * half, half), half), :]
        chip_sum[n, chip] = own + core_in[n]
        for offset in range(1, chips):
            chip_copy(n, offset).start()

    def update(n):
        for offset in range(1, chips):
            chip_arrival(n, offset).wait_recv()
        summed = chip_sum[n, 0]
        for index in range(1, chips):
            summed = summed + chip_sum[n, index]
        old = v_all[lax.div(n, per_step), lax.rem(n, per_step), pl.ds(pl.multiple_of(core * half, half), half)]
        fresh[n] = old + scene_rate * summed
        move_copy(n).start()

    def forward(n):
        move_copy(n).wait_recv()
        forward_copy(n).start()

    def take_first(c):
        for load in first_loads(c):
            load.wait()
        v_all[0, c] = v_first[pl.ds(pl.multiple_of(c * CHUNK, CHUNK), CHUNK), :].T

    def tick(t, carry):
        place_in_step = lax.rem(t, per_step)

        @pl.when(place_in_step == 0)
        def _():
            add_pixel_grad(t - 1, 0, pixels)
            add_cores(t - 1)
            begin_step(lax.div(t, per_step))

        @pl.when(t < per_step)
        def _():
            take_first(t)

        @pl.when(t >= per_step)
        def _():
            forward_arrival(t - per_step).wait_recv()

        @pl.when(place_in_step < pair)
        def _():
            misfits(t)

        @pl.when(place_in_step >= pair)
        def _():
            turn = lax.rem(place_in_step, pair)
            misfits(t)
            add_pixel_grad(t - turn - 1, turn * part, part)

        @pl.when(place_in_step != 0)
        def _():
            add_cores(t - 1)

        stage(t - LAG_FORWARD, forward)
        scene_grad(t)
        core_copy(t).start()
        stage(t - LAG_UPDATE, update)
        return carry

    def late_tick(t, carry):
        stage(t - LAG_UPDATE, update)
        stage(t - LAG_FORWARD, forward)
        return carry

    begin_step(0)
    take_first(0)
    misfits(0)
    scene_grad(0)
    pl.semaphore_wait(barrier, len(partners))
    core_copy(0).start()
    lax.fori_loop(1, total, tick, 0)

    add_pixel_grad(total - 1, 0, pixels)
    add_cores(total - 1)
    for start in range(0, pixels, ROWS):
        rows = pl.ds(start, ROWS)
        pix_out[rows, :] = u_ref[rows, :]
    lax.fori_loop(total, total + LAG_FORWARD, late_tick, 0)

    def finish(c, carry):
        forward_arrival((STEPS - 1) * per_step + c).wait_recv()
        cols = pl.ds(pl.multiple_of(c * CHUNK, CHUNK), CHUNK)
        scene_out[cols, :] = v_all[STEPS, c].T
        return carry

    lax.fori_loop(0, per_step, finish, 0)
    whole = [core_in, fresh, fresh] + [core_in] * (chips - 1)
    for index, like in enumerate(whole):
        pltpu.make_async_copy(like, like, send_sem.at[index]).wait()


def per_device(blk_count, rep_count, pixel_factors, scene_factors, elevations, quality, occupancy):
    pixels, rank = pixel_factors.shape
    acq = scene_factors.shape[0]
    total = STEPS * (acq // CHUNK)
    half = rank // 2
    chips = rep_count // 2
    f32, bf16 = jnp.float32, jnp.bfloat16
    in_vmem = pl.BlockSpec(memory_space=pltpu.VMEM)
    anywhere = pl.BlockSpec(memory_space=pl.ANY)
    dma = pltpu.SemaphoreType.DMA
    return pl.pallas_call(
        functools.partial(kernel, blk_count, rep_count),
        out_shape=(
            pltpu.VMEM((pixels, rank), f32),
            pltpu.VMEM((acq, rank), f32),
        ),
        in_specs=[pl.BlockSpec(memory_space=pltpu.SMEM)] + [anywhere] * 4,
        out_specs=(in_vmem, in_vmem),
        scratch_shapes=[
            pltpu.VMEM(elevations.shape, bf16),
            pltpu.VMEM(quality.shape, bf16),
            pltpu.VMEM((pixels, rank), f32),
            pltpu.VMEM((2 * pixels, rank), bf16),
            pltpu.VMEM((2 * rank, pixels), bf16),
            pltpu.VMEM((acq, rank), f32),
            pltpu.VMEM((STEPS + 1, acq // CHUNK, rank, CHUNK), f32),
            pltpu.VMEM((acq, rank), bf16),
            pltpu.VMEM((acq, rank), bf16),
            pltpu.VMEM((pixels, acq), bf16),
            pltpu.VMEM((pixels, acq), bf16),
            pltpu.VMEM((total, rank, CHUNK), f32),
            pltpu.VMEM((total, half, CHUNK), f32),
            pltpu.VMEM((total, chips, half, CHUNK), f32),
            pltpu.VMEM((total, half, CHUNK), f32),
            dma((1,)),
            dma((3, acq // CHUNK)),
            dma((2, STEPS)),
            dma((2 + chips,)),
            dma((total,)),
            dma((total, chips)),
            dma((total,)),
            dma((total,)),
        ],
        compiler_params=pltpu.CompilerParams(
            collective_id=0, has_side_effects=True, vmem_limit_bytes=VMEM_BYTES
        ),
        cost_estimate=pl.CostEstimate(
            flops=18 * STEPS * pixels * acq * rank, bytes_accessed=12 * 1024 * 1024, transcendentals=0
        ),
    )(occupancy.T, pixel_factors, scene_factors, elevations, quality)


def solution(mesh):
    in_specs = (
        P(("blk", "rep"), None),
        P("blk", None),
        P(None, ("blk", "rep"), None),
        P(None, ("blk", "rep"), None),
        P(None, ("blk", "rep")),
    )
    out_specs = (P(("blk", "rep"), None), P("blk", None))
    return jax.shard_map(
        functools.partial(per_device, mesh.shape["blk"], mesh.shape["rep"]),
        mesh=mesh, in_specs=in_specs, out_specs=out_specs, check_vma=False,
    )
```

```python
import functools

import jax
import jax.numpy as jnp
from jax import lax
from jax.experimental import pallas as pl
from jax.experimental.pallas import tpu as pltpu
from jax.sharding import PartitionSpec as P

MESH = pl.DeviceIdType.MESH
STEPS = 3
CHUNK = 128
PAIR = 256
ROWS = 256
BAND = 128
VMEM_BYTES = 62 * 1024 * 1024
LAG_UPDATE = 2
LAG_SPREAD = 5
LAG_FORWARD = 6


def split(value):
    high = value.astype(jnp.bfloat16)
    return high, (value - high.astype(jnp.float32)).astype(jnp.bfloat16)


def dot(left, right):
    return jnp.dot(left, right, preferred_element_type=jnp.float32)


def kernel(
    blk_count, rep_count,
    occ_ref, pix_ref, scene_ref, elev_ref, qual_ref, pix_out, scene_out,
    elev, qual, u_ref, u_parts, ut_parts, v_first, v_all, v_high, v_low, m_high, m_low,
    grad, core_in, summed, chip_in, fresh,
    load_sem, first_sem, tile_sem, send_sem, core_recv, chip_recv, spread_recv, move_recv, fwd_recv,
):
    pixels, rank = pix_ref.shape
    acq = scene_ref.shape[0]
    per_step = acq // CHUNK
    total = STEPS * per_step
    half = rank // 2
    chips = rep_count // 2
    share = half // chips
    pixel_rate = 8.0 / acq
    scene_rate = 8.0 / (pixels * rep_count)

    group = lax.axis_index("blk")
    rep = lax.axis_index("rep")
    core = lax.rem(rep, 2)
    chip = lax.div(rep, 2)
    other_core = chip * 2 + 1 - core

    def at_blk(shift):
        return lax.rem(group + shift + blk_count, blk_count)

    barrier = pltpu.get_barrier_semaphore()
    partners = [(group, other_core)]
    for offset in range(1, chips):
        partners.append((group, lax.rem(chip + offset, chips) * 2 + core))
    for shift in (-1, 1, STEPS - 1, 1 - STEPS):
        partners.append((at_blk(shift), rep))
    for partner in partners:
        pl.semaphore_signal(barrier, inc=1, device_id=partner, device_id_type=MESH)

    load_u = pltpu.make_async_copy(pix_ref, u_ref, load_sem.at[0])
    load_u.start()

    def first_loads(c):
        cols = pl.ds(pl.multiple_of(c * CHUNK, CHUNK), CHUNK)
        return (
            pltpu.make_async_copy(scene_ref.at[cols], v_first.at[cols], first_sem.at[0, c]),
            pltpu.make_async_copy(elev_ref.at[0, :, cols], elev.at[0, :, cols], first_sem.at[1, c]),
            pltpu.make_async_copy(qual_ref.at[0, :, cols], qual.at[0, :, cols], first_sem.at[2, c]),
        )

    for c in range(per_step):
        for load in first_loads(c):
            load.start()

    def tile_loads(step):
        return (
            pltpu.make_async_copy(elev_ref.at[step], elev.at[step], tile_sem.at[0, step]),
            pltpu.make_async_copy(qual_ref.at[step], qual.at[step], tile_sem.at[1, step]),
        )


    load_u.wait()

    def core_copy(n):
        return pltpu.make_async_remote_copy(
            src_ref=grad.at[n, pl.ds(pl.multiple_of((1 - core) * half, half), half)],
            dst_ref=core_in.at[n],
            send_sem=send_sem.at[0], recv_sem=core_recv.at[n],
            device_id=(group, other_core), device_id_type=MESH,
        )

    def peer(offset):
        return lax.rem(chip + offset, chips)

    def chip_copy(n, offset):
        rows = pl.ds(pl.multiple_of(peer(offset) * share, share), share)
        return pltpu.make_async_remote_copy(
            src_ref=summed.at[n, rows], dst_ref=chip_in.at[n, chip],
            send_sem=send_sem.at[2 + offset], recv_sem=chip_recv.at[n, chip],
            device_id=(group, peer(offset) * 2 + core), device_id_type=MESH,
        )

    def chip_arrival(n, offset):
        return pltpu.make_async_remote_copy(
            src_ref=chip_in.at[n, peer(offset)], dst_ref=chip_in.at[n, peer(offset)],
            send_sem=send_sem.at[2 + offset], recv_sem=chip_recv.at[n, peer(offset)],
            device_id=(group, peer(offset) * 2 + core), device_id_type=MESH,
        )

    def part_place(n, owner):
        start = core * half + owner * share
        return v_all.at[lax.div(n, per_step) + 1, lax.rem(n, per_step), pl.ds(pl.multiple_of(start, share), share)]

    def spread_copy(n, offset):
        return pltpu.make_async_remote_copy(
            src_ref=part_place(n, chip), dst_ref=part_place(n, chip),
            send_sem=send_sem.at[1 + chips + offset], recv_sem=spread_recv.at[n, chip],
            device_id=(group, peer(offset) * 2 + core), device_id_type=MESH,
        )

    def spread_arrival(n, offset):
        return pltpu.make_async_remote_copy(
            src_ref=part_place(n, peer(offset)), dst_ref=part_place(n, peer(offset)),
            send_sem=send_sem.at[1 + chips + offset], recv_sem=spread_recv.at[n, peer(offset)],
            device_id=(group, peer(offset) * 2 + core), device_id_type=MESH,
        )

    def place(n, side):
        step = lax.div(n, per_step)
        return v_all.at[step + 1, lax.rem(n, per_step), pl.ds(pl.multiple_of(side * half, half), half)]

    def move_copy(n):
        last = lax.div(lax.div(n, per_step), STEPS - 1)
        return pltpu.make_async_remote_copy(
            src_ref=fresh.at[n], dst_ref=part_place(n, chip),
            send_sem=send_sem.at[1], recv_sem=move_recv.at[n],
            device_id=(at_blk(last * STEPS - 1), rep), device_id_type=MESH,
        )

    def forward_copy(n):
        return pltpu.make_async_remote_copy(
            src_ref=place(n, core), dst_ref=place(n, core),
            send_sem=send_sem.at[2], recv_sem=fwd_recv.at[n],
            device_id=(group, other_core), device_id_type=MESH,
        )

    def forward_arrival(n):
        return pltpu.make_async_remote_copy(
            src_ref=place(n, 1 - core), dst_ref=place(n, 1 - core),
            send_sem=send_sem.at[2], recv_sem=fwd_recv.at[n],
            device_id=(group, other_core), device_id_type=MESH,
        )

    def begin_step(step):
        @pl.when(step > 0)
        def _():
            for load in tile_loads(step):
                load.wait()

        @pl.when(step + 1 < STEPS)
        def _():
            for load in tile_loads(step + 1):
                load.start()

        for start in range(0, pixels, ROWS):
            rows = pl.ds(start, ROWS)
            u = u_ref[rows, :]
            high, low = split(u)
            u_parts[0, rows, :] = high
            u_parts[1, rows, :] = low
            high, low = split(u.T)
            ut_parts[pl.ds(0, rank), rows] = high
            ut_parts[pl.ds(rank, rank), rows] = low

    def misfits(n):
        step = lax.div(n, per_step)
        first = pl.multiple_of(lax.rem(n, per_step) * CHUNK, CHUNK)
        cols = pl.ds(first, CHUNK)
        flag = occ_ref[0, step].astype(jnp.float32)
        v = v_all[step, lax.rem(n, per_step)]
        high, low = split(v.T)
        v_high[cols, :] = high
        v_low[cols, :] = low
        high, low = split(v)
        v_cat = jnp.concatenate([high, low], axis=1)
        for start in range(0, pixels, ROWS):
            rows = pl.ds(start, ROWS)
            by_high = dot(u_parts[0, rows, :], v_cat)
            by_low = dot(u_parts[1, rows, :], v_cat)
            predicted = by_high[:, :CHUNK] + (by_high[:, CHUNK:] + by_low[:, :CHUNK] + by_low[:, CHUNK:])
            weight = qual[step, rows, cols].astype(jnp.float32) * flag
            misfit = weight * (elev[step, rows, cols].astype(jnp.float32) - predicted)
            high, low = split(misfit)
            m_high[rows, cols] = high
            m_low[rows, cols] = low

    def scene_grad(n):
        cols = pl.ds(pl.multiple_of(lax.rem(n, per_step) * CHUNK, CHUNK), CHUNK)
        parts = dot(ut_parts[...], jnp.concatenate([m_high[:, cols], m_low[:, cols]], axis=1))
        by_high, by_low = parts[:rank], parts[rank:]
        grad[n] = by_high[:, :CHUNK] + (by_high[:, CHUNK:] + by_low[:, :CHUNK] + by_low[:, CHUNK:])

    def add_pixel_grad(n, begin, count):
        first = pl.multiple_of(lax.rem(n, per_step) * CHUNK + CHUNK - PAIR, PAIR)
        cols = pl.ds(first, PAIR)
        high, low = v_high[cols, :], v_low[cols, :]
        v_cat = jnp.concatenate([high, high, low], axis=0)
        for start in range(0, count, BAND):
            rows = pl.ds(pl.multiple_of(begin + start, BAND), BAND)
            high, low = m_high[rows, cols], m_low[rows, cols]
            u_ref[rows, :] += pixel_rate * dot(jnp.concatenate([high, low, high], axis=1), v_cat)

    def stage(n, body):
        @pl.when(jnp.logical_and(n >= 0, n < total))
        def _():
            body(n)

    def add_cores(n):
        core_copy(n).wait_recv()
        own = grad[n, pl.ds(pl.multiple_of(core * half, half), half), :]
        summed[n] = own + core_in[n]
        for offset in range(1, chips):
            chip_copy(n, offset).start()

    def update(n):
        chip_in[n, chip] = summed[n, pl.ds(pl.multiple_of(chip * share, share), share), :]
        for offset in range(1, chips):
            chip_arrival(n, offset).wait_recv()
        gradient = chip_in[n, 0]
        for index in range(1, chips):
            gradient = gradient + chip_in[n, index]
        start = core * half + chip * share
        old = v_all[lax.div(n, per_step), lax.rem(n, per_step), pl.ds(pl.multiple_of(start, share), share)]
        fresh[n] = old + scene_rate * gradient
        move_copy(n).start()

    def spread(n):
        move_copy(n).wait_recv()
        for offset in range(1, chips):
            spread_copy(n, offset).start()

    def forward(n):
        for offset in range(1, chips):
            spread_arrival(n, offset).wait_recv()
        forward_copy(n).start()

    pair = PAIR // CHUNK
    part = pixels // pair

    def take_first(c):
        for load in first_loads(c):
            load.wait()
        v_all[0, c] = v_first[pl.ds(pl.multiple_of(c * CHUNK, CHUNK), CHUNK), :].T

    def tick(t, carry):
        place_in_step = lax.rem(t, per_step)

        @pl.when(place_in_step == 0)
        def _():
            add_pixel_grad(t - 1, 0, pixels)
            add_cores(t - 1)
            begin_step(lax.div(t, per_step))

        @pl.when(t < per_step)
        def _():
            take_first(t)

        @pl.when(t >= per_step)
        def _():
            forward_arrival(t - per_step).wait_recv()

        @pl.when(place_in_step < pair)
        def _():
            misfits(t)

        @pl.when(place_in_step >= pair)
        def _():
            turn = lax.rem(place_in_step, pair)
            misfits(t)
            add_pixel_grad(t - turn - 1, turn * part, part)

        @pl.when(place_in_step != 0)
        def _():
            add_cores(t - 1)

        stage(t - LAG_SPREAD, spread)
        scene_grad(t)
        core_copy(t).start()
        stage(t - LAG_UPDATE, update)
        stage(t - LAG_FORWARD, forward)
        return carry

    def late_tick(t, carry):
        stage(t - LAG_UPDATE, update)
        stage(t - LAG_SPREAD, spread)
        stage(t - LAG_FORWARD, forward)
        return carry

    begin_step(0)
    take_first(0)
    misfits(0)
    scene_grad(0)
    pl.semaphore_wait(barrier, len(partners))
    core_copy(0).start()
    lax.fori_loop(1, total, tick, 0)

    add_pixel_grad(total - 1, 0, pixels)
    add_cores(total - 1)
    for start in range(0, pixels, ROWS):
        rows = pl.ds(start, ROWS)
        pix_out[rows, :] = u_ref[rows, :]
    lax.fori_loop(total, total + LAG_FORWARD, late_tick, 0)

    def finish(c, carry):
        forward_arrival((STEPS - 1) * per_step + c).wait_recv()
        cols = pl.ds(pl.multiple_of(c * CHUNK, CHUNK), CHUNK)
        scene_out[cols, :] = v_all[STEPS, c].T
        return carry

    lax.fori_loop(0, per_step, finish, 0)
    whole = [core_in, fresh, core_in] + [fresh] * (2 * chips - 2)
    for index, like in enumerate(whole):
        pltpu.make_async_copy(like, like, send_sem.at[index]).wait()


def per_device(blk_count, rep_count, pixel_factors, scene_factors, elevations, quality, occupancy):
    pixels, rank = pixel_factors.shape
    acq = scene_factors.shape[0]
    total = STEPS * (acq // CHUNK)
    half = rank // 2
    chips = rep_count // 2
    share = half // chips
    f32, bf16 = jnp.float32, jnp.bfloat16
    in_vmem = pl.BlockSpec(memory_space=pltpu.VMEM)
    anywhere = pl.BlockSpec(memory_space=pl.ANY)
    dma = pltpu.SemaphoreType.DMA
    return pl.pallas_call(
        functools.partial(kernel, blk_count, rep_count),
        out_shape=(
            pltpu.VMEM((pixels, rank), f32),
            pltpu.VMEM((acq, rank), f32),
        ),
        in_specs=[pl.BlockSpec(memory_space=pltpu.SMEM)] + [anywhere] * 4,
        out_specs=(in_vmem, in_vmem),
        scratch_shapes=[
            pltpu.VMEM(elevations.shape, bf16),
            pltpu.VMEM(quality.shape, bf16),
            pltpu.VMEM((pixels, rank), f32),
            pltpu.VMEM((2, pixels, rank), bf16),
            pltpu.VMEM((2 * rank, pixels), bf16),
            pltpu.VMEM((acq, rank), f32),
            pltpu.VMEM((STEPS + 1, acq // CHUNK, rank, CHUNK), f32),
            pltpu.VMEM((acq, rank), bf16),
            pltpu.VMEM((acq, rank), bf16),
            pltpu.VMEM((pixels, acq), bf16),
            pltpu.VMEM((pixels, acq), bf16),
            pltpu.VMEM((total, rank, CHUNK), f32),
            pltpu.VMEM((total, half, CHUNK), f32),
            pltpu.VMEM((total, half, CHUNK), f32),
            pltpu.VMEM((total, chips, half // chips, CHUNK), f32),
            pltpu.VMEM((total, half // chips, CHUNK), f32),
            dma((1,)),
            dma((3, acq // CHUNK)),
            dma((2, STEPS)),
            dma((1 + 2 * chips,)),
            dma((total,)),
            dma((total, chips)),
            dma((total, chips)),
            dma((total,)),
            dma((total,)),
        ],
        compiler_params=pltpu.CompilerParams(
            collective_id=0, has_side_effects=True, vmem_limit_bytes=VMEM_BYTES
        ),
        cost_estimate=pl.CostEstimate(
            flops=18 * STEPS * pixels * acq * rank, bytes_accessed=12 * 1024 * 1024, transcendentals=0
        ),
    )(occupancy.T, pixel_factors, scene_factors, elevations, quality)


def solution(mesh):
    in_specs = (
        P(("blk", "rep"), None),
        P("blk", None),
        P(None, ("blk", "rep"), None),
        P(None, ("blk", "rep"), None),
        P(None, ("blk", "rep")),
    )
    out_specs = (P(("blk", "rep"), None), P("blk", None))
    return jax.shard_map(
        functools.partial(per_device, mesh.shape["blk"], mesh.shape["rep"]),
        mesh=mesh, in_specs=in_specs, out_specs=out_specs, check_vma=False,
    )
```

```python
import functools

import jax
import jax.numpy as jnp
from jax import lax
from jax.experimental import pallas as pl
from jax.experimental.pallas import tpu as pltpu
from jax.sharding import PartitionSpec as P

MESH = pl.DeviceIdType.MESH
STEPS = 3
CHUNK = 128
PAIR = 256
ROWS = 256
BAND = 128
VMEM_BYTES = 62 * 1024 * 1024
LAG_UPDATE = 3
LAG_FORWARD = 5


def split(value):
    high = value.astype(jnp.bfloat16)
    return high, (value - high.astype(jnp.float32)).astype(jnp.bfloat16)


def dot(left, right):
    return jnp.dot(left, right, preferred_element_type=jnp.float32)


def kernel(
    blk_count, rep_count,
    occ_ref, pix_ref, scene_ref, elev_ref, qual_ref, pix_out, scene_out,
    elev, qual, u_ref, u_parts, ut_parts, v_first, v_all, v_high, v_low, m_high, m_low,
    grad, core_in, chip_sum, fresh,
    load_sem, first_sem, tile_sem, send_sem, core_recv, chip_recv, move_recv, fwd_recv,
):
    pixels, rank = pix_ref.shape
    acq = scene_ref.shape[0]
    per_step = acq // CHUNK
    total = STEPS * per_step
    half = rank // 2
    chips = rep_count // 2
    pixel_rate = 8.0 / acq
    scene_rate = 8.0 / (pixels * rep_count)

    group = lax.axis_index("blk")
    rep = lax.axis_index("rep")
    core = lax.rem(rep, 2)
    chip = lax.div(rep, 2)
    other_core = chip * 2 + 1 - core

    def at_blk(shift):
        return lax.rem(group + shift + blk_count, blk_count)

    barrier = pltpu.get_barrier_semaphore()
    partners = [(group, other_core)]
    for offset in range(1, chips):
        partners.append((group, lax.rem(chip + offset, chips) * 2 + core))
    for shift in (-1, 1, STEPS - 1, 1 - STEPS):
        partners.append((at_blk(shift), rep))
    for partner in partners:
        pl.semaphore_signal(barrier, inc=1, device_id=partner, device_id_type=MESH)

    load_u = pltpu.make_async_copy(pix_ref, u_ref, load_sem.at[0])
    load_u.start()

    def first_loads(c):
        cols = pl.ds(pl.multiple_of(c * CHUNK, CHUNK), CHUNK)
        return (
            pltpu.make_async_copy(scene_ref.at[cols], v_first.at[cols], first_sem.at[0, c]),
            pltpu.make_async_copy(elev_ref.at[0, :, cols], elev.at[0, :, cols], first_sem.at[1, c]),
            pltpu.make_async_copy(qual_ref.at[0, :, cols], qual.at[0, :, cols], first_sem.at[2, c]),
        )

    for load in first_loads(0) + first_loads(1):
        load.start()

    def tile_loads(step):
        return (
            pltpu.make_async_copy(elev_ref.at[step], elev.at[step], tile_sem.at[0, step]),
            pltpu.make_async_copy(qual_ref.at[step], qual.at[step], tile_sem.at[1, step]),
        )


    load_u.wait()
    for c in range(2, per_step):
        for load in first_loads(c):
            load.start()

    def core_copy(n):
        return pltpu.make_async_remote_copy(
            src_ref=grad.at[n, pl.ds(pl.multiple_of((1 - core) * half, half), half)],
            dst_ref=core_in.at[n],
            send_sem=send_sem.at[0], recv_sem=core_recv.at[n],
            device_id=(group, other_core), device_id_type=MESH,
        )

    def chip_copy(n, offset):
        return pltpu.make_async_remote_copy(
            src_ref=chip_sum.at[n, chip], dst_ref=chip_sum.at[n, chip],
            send_sem=send_sem.at[2 + offset], recv_sem=chip_recv.at[n, chip],
            device_id=(group, lax.rem(chip + offset, chips) * 2 + core), device_id_type=MESH,
        )

    def chip_arrival(n, offset):
        sender = lax.rem(chip + offset, chips)
        return pltpu.make_async_remote_copy(
            src_ref=chip_sum.at[n, sender], dst_ref=chip_sum.at[n, sender],
            send_sem=send_sem.at[2 + offset], recv_sem=chip_recv.at[n, sender],
            device_id=(group, sender * 2 + core), device_id_type=MESH,
        )

    def place(n, side):
        step = lax.div(n, per_step)
        return v_all.at[step + 1, lax.rem(n, per_step), pl.ds(pl.multiple_of(side * half, half), half)]

    def move_copy(n):
        last = lax.div(lax.div(n, per_step), STEPS - 1)
        return pltpu.make_async_remote_copy(
            src_ref=fresh.at[n], dst_ref=place(n, core),
            send_sem=send_sem.at[1], recv_sem=move_recv.at[n],
            device_id=(at_blk(last * STEPS - 1), rep), device_id_type=MESH,
        )

    def forward_copy(n):
        return pltpu.make_async_remote_copy(
            src_ref=place(n, core), dst_ref=place(n, core),
            send_sem=send_sem.at[2], recv_sem=fwd_recv.at[n],
            device_id=(group, other_core), device_id_type=MESH,
        )

    def forward_arrival(n):
        return pltpu.make_async_remote_copy(
            src_ref=place(n, 1 - core), dst_ref=place(n, 1 - core),
            send_sem=send_sem.at[2], recv_sem=fwd_recv.at[n],
            device_id=(group, other_core), device_id_type=MESH,
        )

    def begin_step(step):
        @pl.when(step > 0)
        def _():
            for load in tile_loads(step):
                load.wait()

        @pl.when(step + 1 < STEPS)
        def _():
            for load in tile_loads(step + 1):
                load.start()

        for start in range(0, pixels, ROWS):
            rows = pl.ds(start, ROWS)
            u = u_ref[rows, :]
            high, low = split(u)
            u_parts[0, rows, :] = high
            u_parts[1, rows, :] = low
            high, low = split(u.T)
            ut_parts[pl.ds(0, rank), rows] = high
            ut_parts[pl.ds(rank, rank), rows] = low

    def misfits(n):
        step = lax.div(n, per_step)
        first = pl.multiple_of(lax.rem(n, per_step) * CHUNK, CHUNK)
        cols = pl.ds(first, CHUNK)
        flag = occ_ref[0, step].astype(jnp.float32)
        v = v_all[step, lax.rem(n, per_step)]
        high, low = split(v.T)
        v_high[cols, :] = high
        v_low[cols, :] = low
        high, low = split(v)
        v_cat = jnp.concatenate([high, low], axis=1)
        for start in range(0, pixels, ROWS):
            rows = pl.ds(start, ROWS)
            by_high = dot(u_parts[0, rows, :], v_cat)
            by_low = dot(u_parts[1, rows, :], v_cat)
            predicted = by_high[:, :CHUNK] + (by_high[:, CHUNK:] + by_low[:, :CHUNK] + by_low[:, CHUNK:])
            weight = qual[step, rows, cols].astype(jnp.float32) * flag
            misfit = weight * (elev[step, rows, cols].astype(jnp.float32) - predicted)
            high, low = split(misfit)
            m_high[rows, cols] = high
            m_low[rows, cols] = low

    def scene_grad(n):
        cols = pl.ds(pl.multiple_of(lax.rem(n, per_step) * CHUNK, CHUNK), CHUNK)
        parts = dot(ut_parts[...], jnp.concatenate([m_high[:, cols], m_low[:, cols]], axis=1))
        by_high, by_low = parts[:rank], parts[rank:]
        grad[n] = by_high[:, :CHUNK] + (by_high[:, CHUNK:] + by_low[:, :CHUNK] + by_low[:, CHUNK:])

    def add_pixel_grad(n, begin, count):
        first = pl.multiple_of(lax.rem(n, per_step) * CHUNK + CHUNK - PAIR, PAIR)
        cols = pl.ds(first, PAIR)
        high, low = v_high[cols, :], v_low[cols, :]
        v_cat = jnp.concatenate([high, high, low], axis=0)
        for start in range(0, count, BAND):
            rows = pl.ds(pl.multiple_of(begin + start, BAND), BAND)
            high, low = m_high[rows, cols], m_low[rows, cols]
            u_ref[rows, :] += pixel_rate * dot(jnp.concatenate([high, low, high], axis=1), v_cat)

    def stage(n, body):
        @pl.when(jnp.logical_and(n >= 0, n < total))
        def _():
            body(n)

    def add_cores(n):
        core_copy(n).wait_recv()
        own = grad[n, pl.ds(pl.multiple_of(core * half, half), half), :]
        chip_sum[n, chip] = own + core_in[n]
        for offset in range(1, chips):
            chip_copy(n, offset).start()

    def update(n):
        for offset in range(1, chips):
            chip_arrival(n, offset).wait_recv()
        summed = chip_sum[n, 0]
        for index in range(1, chips):
            summed = summed + chip_sum[n, index]
        old = v_all[lax.div(n, per_step), lax.rem(n, per_step), pl.ds(pl.multiple_of(core * half, half), half)]
        fresh[n] = old + scene_rate * summed
        move_copy(n).start()

    def forward(n):
        move_copy(n).wait_recv()
        forward_copy(n).start()

    pair = PAIR // CHUNK
    part = pixels // pair

    def take_first(c):
        for load in first_loads(c):
            load.wait()
        v_all[0, c] = v_first[pl.ds(pl.multiple_of(c * CHUNK, CHUNK), CHUNK), :].T

    def tick(t, carry):
        place_in_step = lax.rem(t, per_step)

        @pl.when(place_in_step == 0)
        def _():
            add_pixel_grad(t - 1, 0, pixels)
            add_cores(t - 1)
            begin_step(lax.div(t, per_step))

        @pl.when(t < per_step)
        def _():
            take_first(t)

        @pl.when(t >= per_step)
        def _():
            forward_arrival(t - per_step).wait_recv()

        @pl.when(place_in_step < pair)
        def _():
            misfits(t)

        @pl.when(place_in_step >= pair)
        def _():
            turn = lax.rem(place_in_step, pair)
            misfits(t)
            add_pixel_grad(t - turn - 1, turn * part, part)

        @pl.when(place_in_step != 0)
        def _():
            add_cores(t - 1)

        scene_grad(t)
        core_copy(t).start()
        stage(t - LAG_UPDATE, update)
        stage(t - LAG_FORWARD, forward)
        return carry

    def late_tick(t, carry):
        stage(t - LAG_UPDATE, update)
        stage(t - LAG_FORWARD, forward)
        return carry

    begin_step(0)
    take_first(0)
    misfits(0)
    scene_grad(0)
    pl.semaphore_wait(barrier, len(partners))
    core_copy(0).start()
    lax.fori_loop(1, total, tick, 0)

    add_pixel_grad(total - 1, 0, pixels)
    add_cores(total - 1)
    for start in range(0, pixels, ROWS):
        rows = pl.ds(start, ROWS)
        pix_out[rows, :] = u_ref[rows, :]
    lax.fori_loop(total, total + LAG_FORWARD, late_tick, 0)

    def finish(c, carry):
        forward_arrival((STEPS - 1) * per_step + c).wait_recv()
        cols = pl.ds(pl.multiple_of(c * CHUNK, CHUNK), CHUNK)
        scene_out[cols, :] = v_all[STEPS, c].T
        return carry

    lax.fori_loop(0, per_step, finish, 0)
    whole = [core_in, fresh, fresh] + [core_in] * (chips - 1)
    for index, like in enumerate(whole):
        pltpu.make_async_copy(like, like, send_sem.at[index]).wait()


def per_device(blk_count, rep_count, pixel_factors, scene_factors, elevations, quality, occupancy):
    pixels, rank = pixel_factors.shape
    acq = scene_factors.shape[0]
    total = STEPS * (acq // CHUNK)
    half = rank // 2
    chips = rep_count // 2
    f32, bf16 = jnp.float32, jnp.bfloat16
    in_vmem = pl.BlockSpec(memory_space=pltpu.VMEM)
    anywhere = pl.BlockSpec(memory_space=pl.ANY)
    dma = pltpu.SemaphoreType.DMA
    return pl.pallas_call(
        functools.partial(kernel, blk_count, rep_count),
        out_shape=(
            pltpu.VMEM((pixels, rank), f32),
            pltpu.VMEM((acq, rank), f32),
        ),
        in_specs=[pl.BlockSpec(memory_space=pltpu.SMEM)] + [anywhere] * 4,
        out_specs=(in_vmem, in_vmem),
        scratch_shapes=[
            pltpu.VMEM(elevations.shape, bf16),
            pltpu.VMEM(quality.shape, bf16),
            pltpu.VMEM((pixels, rank), f32),
            pltpu.VMEM((2, pixels, rank), bf16),
            pltpu.VMEM((2 * rank, pixels), bf16),
            pltpu.VMEM((acq, rank), f32),
            pltpu.VMEM((STEPS + 1, acq // CHUNK, rank, CHUNK), f32),
            pltpu.VMEM((acq, rank), bf16),
            pltpu.VMEM((acq, rank), bf16),
            pltpu.VMEM((pixels, acq), bf16),
            pltpu.VMEM((pixels, acq), bf16),
            pltpu.VMEM((total, rank, CHUNK), f32),
            pltpu.VMEM((total, half, CHUNK), f32),
            pltpu.VMEM((total, chips, half, CHUNK), f32),
            pltpu.VMEM((total, half, CHUNK), f32),
            dma((1,)),
            dma((3, acq // CHUNK)),
            dma((2, STEPS)),
            dma((2 + chips,)),
            dma((total,)),
            dma((total, chips)),
            dma((total,)),
            dma((total,)),
        ],
        compiler_params=pltpu.CompilerParams(
            collective_id=0, has_side_effects=True, vmem_limit_bytes=VMEM_BYTES
        ),
        cost_estimate=pl.CostEstimate(
            flops=18 * STEPS * pixels * acq * rank, bytes_accessed=12 * 1024 * 1024, transcendentals=0
        ),
    )(occupancy.T, pixel_factors, scene_factors, elevations, quality)


def solution(mesh):
    in_specs = (
        P(("blk", "rep"), None),
        P("blk", None),
        P(None, ("blk", "rep"), None),
        P(None, ("blk", "rep"), None),
        P(None, ("blk", "rep")),
    )
    out_specs = (P(("blk", "rep"), None), P("blk", None))
    return jax.shard_map(
        functools.partial(per_device, mesh.shape["blk"], mesh.shape["rep"]),
        mesh=mesh, in_specs=in_specs, out_specs=out_specs, check_vma=False,
    )
```
